256 devices in a mesh: dom: 64 (over z, y, core), rep: 4 (over x).
Axes of the slice: x: 4, y: 4, z: 8, core: 2. Of those that a mesh axis runs over, the one named last changes fastest.
Arguments:
- adjacency: bfloat16 [131072, 2048], P('dom'), may hold values from -0.09375 to 0.09375
- grad_out: bfloat16 [4, 131072, 128], P('rep', 'dom'), may hold values from -6 to 6
- row_owner: int32 [131072, 1], P('dom'), may hold values from 0 to 63; in each aligned block of 512 rows (0 to 511, 512 to 1023, ...) at most 16 rows name the same one
- table_slot: int32 [131072], P('dom'), may hold values from 0 to 511
- table_rows: float32 [32768, 128], P('dom'), may hold values from -6 to 6
- row_accumulators: float32 [32768], P('dom'), may hold values from 0.01 to 1
Outputs:
- new_table: float32 [32768, 128], P('dom')
- new_accumulators: float32 [32768], P('dom')
- fresh_rows: bfloat16 [131072, 128], P('dom')
The draws below stay inside these ranges and needn't reach their ends.
Inputs may be any that keep to these rules, and one draw needn't show every extreme that they name: `row_owner`: in each aligned block of 512 rows no owner is named by more than 16 rows, a bound that some block reaches.
All inputs are finite; a program needn't handle non-finite values.
Results may differ from the reference program's by a relative error of at most 0.009.
Values may be sent and summed in bfloat16 or wider, within the bound.
No kernel may reach another device: no remote copies, remote signals or barrier semaphores. Data moves between devices by JAX's collectives and lax.ppermute only.
A program may use at most 64 MiB of HBM per device.

```python
import math
import jax
import jax.numpy as jnp
import numpy as np
from jax import lax

D = 128
LAYERS = 3
ROWS = 2048
SHARD = 512
CAP = 16
TOTAL_ROWS = 131072
TABLE = 32768
N_DOM = 64
N_REP = 4


def plant(values, rng, smallest, top_value):
    spot = [jax.random.randint(jax.random.fold_in(rng, axis), (), 0, length) for axis, length in enumerate(values.shape)]
    widest = values.shape.index(max(values.shape))
    next_to = spot[:widest] + [(spot[widest] + 1) % values.shape[widest]] + spot[widest + 1:]
    return values.at[tuple(spot)].set(smallest).at[tuple(next_to)].set(top_value)


def levels(own_key, dims, split, smallest, largest):
    gain, own = 1.0, jax.random.fold_in(own_key, 6)
    for dim, parts in split:
        draws = jnp.exp(jax.random.uniform(jax.random.fold_in(own, dim), (parts,), jnp.float32, smallest / len(split), largest / len(split)))
        gain = gain * jnp.repeat(draws, dims[dim] // parts).reshape([-1 if axis == dim else 1 for axis in range(len(dims))])
    return gain


def deal_out(key, own, number, rows, number_of, top, limit, skew):
    sequence = jax.random.permutation(key, number_of)
    heavy_load, common = load_shares(number_of, rows * top, limit, skew, True), load_shares(number_of, rows * top, limit, skew, False)
    places = jnp.arange(number_of)

    def named(sizes, rotation):
        used = int((sizes > 0).sum())
        fixed = max(1, used // 4)
        passed = fixed + (places - fixed + rotation * (used - fixed)) % max(1, number_of - fixed)
        return jnp.zeros((number_of,), jnp.int32).at[sequence[jnp.where(places < fixed, places, passed)]].set(jnp.asarray(sizes, jnp.int32))

    sizes = jnp.where(number % 4 == 0, named(heavy_load, number // 4), named(common, number - number // 4 - 1))
    mixed = jax.random.permutation(jax.random.fold_in(own, 3), number_of)
    giver, taker = mixed[0:number_of // 2 * 2:2], mixed[1:number_of // 2 * 2:2]
    room = jnp.minimum(sizes[giver] - 1, limit - sizes[taker]) // 2
    room = jnp.where((giver == sequence[0]) | (taker == sequence[0]) | (sizes[taker] == 0), 0, jnp.maximum(room, 0))
    passed = jax.random.randint(jax.random.fold_in(own, 4), (number_of // 2,), 0, 1 << 20) % (room + 1)
    sizes = sizes.at[giver].add(-passed).at[taker].add(passed)
    items = jnp.searchsorted(jnp.cumsum(sizes), jnp.arange(rows * top), side="right").astype(jnp.int32)
    listing = items.reshape(top, rows).T
    listing = listing[jax.random.permutation(jax.random.fold_in(own, 1), rows)]
    rotation = jax.random.randint(jax.random.fold_in(own, 2), (rows, 1), 0, top)
    return jnp.take_along_axis(listing, (jnp.arange(top)[None, :] + rotation) % top, axis=1)


def load_shares(amount, total, bound, skew, full):
    loads = [(1 << 20) // math.isqrt(rank ** skew) + 1 for rank in range(1, amount + 1)]
    largest = bound if full else min(bound, max(-(-total // amount), total * loads[0] // sum(loads)))
    least = 1 if total - largest >= amount - 1 else 0
    holding, spare = [largest] + [least] * (amount - 1), total - largest - least * (amount - 1)
    while spare > 0:
        candidates = [i for i in range(1, amount) if holding[i] < largest] or [i for i in range(1, amount) if holding[i] < bound]
        pool, left = sum([loads[i] for i in candidates]), spare
        for i in candidates:
            extra = min(bound - holding[i], max(1, left * loads[i] // pool), spare)
            holding[i] = holding[i] + extra
            spare = spare - extra
    return np.array(holding)


def bell_draw(key, shape, width, limit, cuts=(), kind=jnp.bfloat16):
    loudness = levels(key, shape, cuts, -0.22, 0.18) if cuts else 1.0
    array = jax.random.normal(key, shape, jnp.float32) * width * loudness
    return jnp.minimum(jnp.maximum(array, -limit), limit).astype(kind)


def setup_inputs(seed: int = 0) -> dict:
    key_list = jax.random.split(jax.random.key(seed), 7)
    adjacency = bell_draw(key_list[0], (TOTAL_ROWS, ROWS), (2 * ROWS) ** -0.5, 0.09375, ((0, 64),))
    grad_out = bell_draw(key_list[1], (N_REP, TOTAL_ROWS, D), 1.0, 6.0, ((0, 4), (1, 64)))
    row_owner_keys = jax.random.split(jax.random.fold_in(key_list[2], 1), TOTAL_ROWS // (ROWS // N_REP))
    row_owner_turns = jax.random.permutation(jax.random.fold_in(key_list[2], 3), TOTAL_ROWS // (ROWS // N_REP))
    row_owner = jax.vmap(lambda own, number: deal_out(jax.random.fold_in(key_list[2], 2), own, number, ROWS // N_REP, N_DOM, 1, CAP, 2))(row_owner_keys, row_owner_turns).reshape((TOTAL_ROWS, 1))
    table_slot = plant(jax.random.randint(key_list[3], (TOTAL_ROWS,), 0, SHARD), jax.random.fold_in(key_list[3], 1), 0, SHARD - 1).astype(jnp.int32)
    table_rows = bell_draw(key_list[4], (TABLE, D), 1.0, 6.0, ((0, 64),), jnp.float32)
    row_accumulators = jnp.clip(jnp.exp(math.log(1.0) - 4.6051702 * jax.random.uniform(key_list[5], (TABLE,), jnp.float32) ** levels(key_list[5], (TABLE,), ((0, 64),), -0.2, 0.2)), 0.01, 1.0)
    return dict(adjacency=adjacency, grad_out=grad_out, row_owner=row_owner, table_slot=table_slot, table_rows=table_rows, row_accumulators=row_accumulators)


def adjoint(tile, piece):
    return lax.dot_general(tile, piece, (((0,), (0,)), ((), ())), preferred_element_type=jnp.float32)

def reference(adjacency, grad_out, row_owner, table_slot, table_rows, row_accumulators):
    tiles = adjacency.reshape(N_DOM, ROWS, ROWS)
    grads = grad_out.reshape(N_REP, N_DOM, ROWS, D).transpose(1, 2, 0, 3).reshape(N_DOM, ROWS, N_REP * D)

    def one_part(pair):
        tile, state = pair
        total = state.astype(jnp.float32)
        for layer in range(LAYERS):
            state = adjoint(tile, state).astype(jnp.bfloat16)
            total = total + state.astype(jnp.float32)
        term = total / jnp.float32(LAYERS + 1)
        return lax.optimization_barrier(jnp.sum(term.reshape(ROWS, N_REP, D), axis=1))
    row_grad = lax.map(one_part, (tiles, grads)).reshape(N_DOM * ROWS, D)
    target = (row_owner[:, 0] * SHARD + table_slot).astype(jnp.int32)
    table_grad = jax.ops.segment_sum(row_grad, target, num_segments=N_DOM * SHARD)
    new_accumulators = row_accumulators + lax.optimization_barrier(jnp.mean(table_grad * table_grad, axis=1))
    new_table = table_rows - 0.5 * table_grad / jnp.sqrt(new_accumulators)[:, None]
    fresh_rows = new_table[target].astype(jnp.bfloat16)
    return (new_table, new_accumulators, fresh_rows)
```

```python
import jax
import jax.numpy as jnp
from jax import lax
from jax.sharding import PartitionSpec as P

LAYERS = 3
LEARN_RATE = 0.5
LANES = 128
SPARE = 8


def adjoint(tile, piece):
    return lax.dot_general(
        tile, piece, (((0,), (0,)), ((), ())), preferred_element_type=jnp.float32
    )


def propagate(adjacency, start):
    state = start
    total = state.astype(jnp.float32)
    for layer in range(LAYERS):
        state = adjoint(adjacency, state).astype(jnp.bfloat16)
        total = total + state.astype(jnp.float32)
    return total / jnp.float32(LAYERS + 1)


def one_hot(values, count, axis):
    shape = (count, values.shape[0]) if axis == 0 else (values.shape[0], count)
    ids = lax.broadcasted_iota(jnp.int32, shape, axis)
    return (jnp.expand_dims(values, axis) == ids).astype(jnp.bfloat16)


def plan(owners, peers, capacity):
    count = owners.shape[0]
    owner_hot = one_hot(owners, peers, 1)
    lower = (
        lax.broadcasted_iota(jnp.int32, (count, count), 0)
        >= lax.broadcasted_iota(jnp.int32, (count, count), 1)
    ).astype(jnp.bfloat16)
    running = jnp.dot(lower, owner_hot, preferred_element_type=jnp.float32)
    ranks = jnp.sum(owner_hot.astype(jnp.float32) * (running - 1.0), axis=1).astype(jnp.int32)
    dispatch = one_hot(owners * capacity + ranks, peers * capacity, 1)
    return owner_hot, ranks, dispatch


def slot_rows(owner_hot, ranks, slots, capacity):
    lane = lax.broadcasted_iota(jnp.int32, (1, LANES), 1)
    part = jnp.where(lane < capacity, slots[:, None] // 16, slots[:, None] % 16)
    hit = (lane < 2 * capacity) & (ranks[:, None] == lane % capacity)
    spread = jnp.where(hit, part, 0).astype(jnp.bfloat16)
    rows = lax.dot_general(
        owner_hot, spread, (((0,), (0,)), ((), ())), preferred_element_type=jnp.float32
    )
    return rows.astype(jnp.bfloat16)


def on_device(adjacency, grad_out, row_owner, table_slot, table_rows, row_accumulators):
    peers = lax.axis_size("dom")
    replicas = lax.axis_size("rep")
    rows = adjacency.shape[0]
    width = grad_out.shape[2]
    shard = table_rows.shape[0]
    quarter = rows // replicas
    capacity = max(2, 2 * quarter // peers)
    here = lax.axis_index("rep") * quarter
    owners = lax.dynamic_slice(row_owner[:, 0], (here,), (quarter,))
    slots = lax.dynamic_slice(table_slot, (here,), (quarter,))
    owner_hot, ranks, dispatch = plan(owners, peers, capacity)
    slot_row = slot_rows(owner_hot, ranks, slots, capacity)

    term = propagate(adjacency, grad_out[0]).astype(jnp.bfloat16)
    terms = lax.all_to_all(
        term.reshape(replicas, quarter, width), "rep", split_axis=0, concat_axis=0, tiled=True
    )
    row_grad = jnp.sum(terms.astype(jnp.float32), axis=0).astype(jnp.bfloat16)

    outgoing = lax.dot_general(
        dispatch, row_grad, (((0,), (0,)), ((), ())), preferred_element_type=jnp.float32
    ).astype(jnp.bfloat16)
    message = jnp.concatenate(
        [
            outgoing.reshape(peers, capacity, width),
            jnp.broadcast_to(slot_row[:, None, :], (peers, SPARE, LANES)),
        ],
        axis=1,
    )
    incoming = lax.all_to_all(message, "dom", split_axis=0, concat_axis=0, tiled=True)
    got = incoming[:, capacity, : 2 * capacity].astype(jnp.int32)
    got_slots = (got[:, :capacity] * 16 + got[:, capacity:]).reshape(-1)
    receiver = one_hot(got_slots, shard, 0)
    partial = jnp.dot(
        receiver,
        incoming[:, :capacity].reshape(peers * capacity, width),
        preferred_element_type=jnp.float32,
    ).astype(jnp.bfloat16)
    partials = lax.all_to_all(
        jnp.broadcast_to(partial, (replicas, shard, width)),
        "rep", split_axis=0, concat_axis=0, tiled=True,
    )
    table_grad = jnp.sum(partials.astype(jnp.float32), axis=0)
    new_accumulators = row_accumulators + jnp.mean(table_grad * table_grad, axis=1)
    new_table = table_rows - LEARN_RATE * table_grad / jnp.sqrt(new_accumulators)[:, None]

    answer = lax.dot_general(
        receiver, new_table.astype(jnp.bfloat16), (((0,), (0,)), ((), ())),
        preferred_element_type=jnp.float32,
    ).astype(jnp.bfloat16)
    returned = lax.all_to_all(
        answer.reshape(peers, capacity, width), "dom", split_axis=0, concat_axis=0, tiled=True
    )
    fresh = jnp.dot(
        dispatch, returned.reshape(peers * capacity, width), preferred_element_type=jnp.float32
    ).astype(jnp.bfloat16)
    fresh_rows = lax.all_to_all(
        jnp.broadcast_to(fresh, (replicas, quarter, width)),
        "rep", split_axis=0, concat_axis=0, tiled=True,
    ).reshape(rows, width)
    return (new_table, new_accumulators, fresh_rows)


def solution(mesh):
    return jax.shard_map(
        on_device,
        mesh=mesh,
        in_specs=(
            P("dom", None),
            P("rep", "dom", None),
            P("dom", None),
            P("dom"),
            P("dom", None),
            P("dom"),
        ),
        out_specs=(P("dom", None), P("dom"), P("dom", None)),
        check_vma=False,
    )
```

```python
import jax
import jax.numpy as jnp
from jax import lax
from jax.experimental import pallas as pl
from jax.experimental.pallas import tpu as pltpu
from jax.sharding import PartitionSpec as P

LAYERS = 3
LEARN_RATE = 0.5
LANES = 128
BLOCKS = 8


def propagate_kernel(me_ref, tile_hbm, grad_ref, *refs):
    outs = refs[:-4]
    tile, state, total, arrived = refs[-4:]
    blocks = arrived.shape[0]
    replicas = len(outs)
    rows = tile.shape[0]
    depth = rows // blocks
    quarter = rows // replicas
    copies = []
    for block in range(blocks):
        part = pl.ds(block * depth, depth)
        copies.append(
            pltpu.make_async_copy(tile_hbm.at[part], tile.at[part], arrived.at[block])
        )
        copies[-1].start()
    first = grad_ref[...].T
    state[...] = first
    for block in range(blocks):
        copies[block].wait()
        part = slice(block * depth, (block + 1) * depth)
        product = jnp.dot(state[:, part], tile[part, :], preferred_element_type=jnp.float32)
        if block == 0:
            total[...] = product
        else:
            total[...] += product
    second = total[...].astype(jnp.bfloat16)
    total[...] = first.astype(jnp.float32) + second.astype(jnp.float32)
    state[...] = second
    third = [
        jnp.dot(
            state[...],
            tile[:, part * quarter : (part + 1) * quarter],
            preferred_element_type=jnp.float32,
        ).astype(jnp.bfloat16)
        for part in range(replicas)
    ]
    for part in range(replicas):
        lanes = slice(part * quarter, (part + 1) * quarter)
        state[:, lanes] = third[part]
    for step in range(replicas):
        start = lax.rem(me_ref[0] + step, replicas) * quarter
        lanes = pl.ds(pl.multiple_of(start, quarter), quarter)
        last = jnp.dot(state[...], tile[:, lanes], preferred_element_type=jnp.float32)
        term = (
            total[:, lanes]
            + state[:, lanes].astype(jnp.float32)
            + last.astype(jnp.bfloat16).astype(jnp.float32)
        ) / jnp.float32(LAYERS + 1)
        outs[step][...] = term.astype(jnp.bfloat16).T


def propagate(adjacency, start, me, replicas):
    rows, width = start.shape
    whole = pl.BlockSpec(memory_space=pltpu.VMEM)
    piece = jax.ShapeDtypeStruct((rows // replicas, width), jnp.bfloat16)
    return pl.pallas_call(
        propagate_kernel,
        out_shape=[piece] * replicas,
        in_specs=[
            pl.BlockSpec(memory_space=pltpu.SMEM),
            pl.BlockSpec(memory_space=pltpu.HBM),
            whole,
        ],
        out_specs=[whole] * replicas,
        scratch_shapes=[
            pltpu.VMEM((rows, rows), jnp.bfloat16),
            pltpu.VMEM((width, rows), jnp.bfloat16),
            pltpu.VMEM((width, rows), jnp.float32),
            pltpu.SemaphoreType.DMA((BLOCKS,)),
        ],
        compiler_params=pltpu.CompilerParams(vmem_limit_bytes=32 * 1024 * 1024),
        cost_estimate=pl.CostEstimate(
            flops=2 * LAYERS * rows * rows * width,
            bytes_accessed=2 * rows * rows + 4 * rows * width,
            transcendentals=0,
        ),
    )(me, adjacency, start)


def send(piece, step, replicas):
    return lax.ppermute(piece, "rep", [(i, (i + step) % replicas) for i in range(replicas)])


def send_order(replicas):
    return sorted(range(1, replicas), key=lambda step: -min(step, replicas - step))


def one_hot(values, count, axis):
    shape = (count, values.shape[0]) if axis == 0 else (values.shape[0], count)
    ids = lax.broadcasted_iota(jnp.int32, shape, axis)
    return (jnp.expand_dims(values, axis) == ids).astype(jnp.bfloat16)


def plan(owners, peers, capacity):
    count = owners.shape[0]
    owner_hot = one_hot(owners, peers, 1)
    lower = (
        lax.broadcasted_iota(jnp.int32, (count, count), 0)
        >= lax.broadcasted_iota(jnp.int32, (count, count), 1)
    ).astype(jnp.bfloat16)
    running = jnp.dot(lower, owner_hot, preferred_element_type=jnp.float32)
    ranks = jnp.sum(owner_hot.astype(jnp.float32) * (running - 1.0), axis=1).astype(jnp.int32)
    dispatch = one_hot(owners * capacity + ranks, peers * capacity, 1)
    return owner_hot, ranks, dispatch


def slot_rows(owner_hot, ranks, slots, capacity):
    lane = lax.broadcasted_iota(jnp.int32, (1, LANES), 1)
    part = jnp.where(lane < capacity, slots[:, None] // 16, slots[:, None] % 16)
    hit = (lane < 2 * capacity) & (ranks[:, None] == lane % capacity)
    spread = jnp.where(hit, part, 0).astype(jnp.bfloat16)
    rows = lax.dot_general(
        owner_hot, spread, (((0,), (0,)), ((), ())), preferred_element_type=jnp.float32
    )
    return rows.astype(jnp.bfloat16)


def on_device(adjacency, grad_out, row_owner, table_slot, table_rows, row_accumulators):
    peers = lax.axis_size("dom")
    replicas = lax.axis_size("rep")
    rows = adjacency.shape[0]
    width = grad_out.shape[2]
    shard = table_rows.shape[0]
    quarter = rows // replicas
    capacity = max(2, 2 * quarter // peers)
    here = lax.axis_index("rep") * quarter
    owners = lax.dynamic_slice(row_owner[:, 0], (here,), (quarter,))
    slots = lax.dynamic_slice(table_slot, (here,), (quarter,))
    owner_hot, ranks, dispatch = plan(owners, peers, capacity)
    slot_row = slot_rows(owner_hot, ranks, slots, capacity)

    me = lax.axis_index("rep")
    terms = propagate(adjacency, grad_out[0], jnp.full((1,), me, jnp.int32), replicas)
    got_terms = [send(terms[step], step, replicas) for step in send_order(replicas)]
    row_grad = terms[0].astype(jnp.float32)
    for piece in got_terms:
        row_grad = row_grad + piece.astype(jnp.float32)
    row_grad = row_grad.astype(jnp.bfloat16)

    outgoing = lax.dot_general(
        dispatch, row_grad, (((0,), (0,)), ((), ())), preferred_element_type=jnp.float32
    ).astype(jnp.bfloat16)
    message = jnp.concatenate(
        [
            outgoing.reshape(peers, capacity // 2, 2, width),
            jnp.broadcast_to(slot_row[:, None, None, :], (peers, 1, 2, LANES)),
        ],
        axis=1,
    )
    incoming = lax.all_to_all(message, "dom", split_axis=0, concat_axis=0, tiled=True)
    got = incoming[:, capacity // 2, 0, : 2 * capacity].astype(jnp.int32)
    got_slots = (got[:, :capacity] * 16 + got[:, capacity:]).reshape(-1)
    receiver = one_hot(got_slots, shard, 0)
    partial = jnp.dot(
        receiver,
        incoming[:, : capacity // 2].reshape(peers * capacity, width),
        preferred_element_type=jnp.float32,
    ).astype(jnp.bfloat16)
    opposite, *beside = [send(partial, step, replicas) for step in send_order(replicas)]
    table_grad = (partial.astype(jnp.float32) + opposite.astype(jnp.float32)) + (
        beside[0].astype(jnp.float32) + beside[1].astype(jnp.float32)
    )
    new_accumulators = row_accumulators + jnp.mean(table_grad * table_grad, axis=1)
    new_table = table_rows - LEARN_RATE * table_grad / jnp.sqrt(new_accumulators)[:, None]

    answer = lax.dot_general(
        receiver, new_table.astype(jnp.bfloat16), (((0,), (0,)), ((), ())),
        preferred_element_type=jnp.float32,
    ).astype(jnp.bfloat16)
    returned = lax.all_to_all(
        answer.reshape(peers, capacity, width), "dom", split_axis=0, concat_axis=0, tiled=True
    )
    fresh = jnp.dot(
        dispatch, returned.reshape(peers * capacity, width), preferred_element_type=jnp.float32
    ).astype(jnp.bfloat16)
    fresh_rows = jnp.zeros((rows, width), jnp.bfloat16)
    for step in [*send_order(replicas), 0]:
        piece = send(fresh, step, replicas) if step else fresh
        source = lax.rem(me + replicas - step, replicas) * quarter
        fresh_rows = lax.dynamic_update_slice(fresh_rows, piece, (source, 0))
    return (new_table, new_accumulators, fresh_rows)


def solution(mesh):
    return jax.shard_map(
        on_device,
        mesh=mesh,
        in_specs=(
            P("dom", None),
            P("rep", "dom", None),
            P("dom", None),
            P("dom"),
            P("dom", None),
            P("dom"),
        ),
        out_specs=(P("dom", None), P("dom"), P("dom", None)),
        check_vma=False,
    )
```

```python
import jax
import jax.numpy as jnp
from jax import lax
from jax.experimental import pallas as pl
from jax.experimental.pallas import tpu as pltpu
from jax.sharding import PartitionSpec as P

LAYERS = 3
LEARN_RATE = 0.5
LANES = 128
BLOCKS = 8
RADIX_BITS = 4
MEBI = 1024 * 1024

VMEM = pl.BlockSpec(memory_space=pltpu.VMEM)
SMEM = pl.BlockSpec(memory_space=pltpu.SMEM)
HBM = pl.BlockSpec(memory_space=pltpu.HBM)
BF16 = jnp.bfloat16
F32 = jnp.float32


def ids(shape, axis):
    return lax.broadcasted_iota(jnp.int32, shape, axis)


def product(left, right):
    return jnp.dot(left, right, preferred_element_type=F32)


def shaped(shape, dtype):
    return jax.ShapeDtypeStruct(shape, dtype)


def call(kernel, out_shape, in_specs, out_specs, scratch=(), mebi=16, flops=0, moved=0):
    return pl.pallas_call(
        kernel,
        out_shape=out_shape,
        in_specs=in_specs,
        out_specs=out_specs,
        scratch_shapes=list(scratch),
        compiler_params=pltpu.CompilerParams(vmem_limit_bytes=mebi * MEBI),
        cost_estimate=pl.CostEstimate(flops=flops, bytes_accessed=moved, transcendentals=0),
    )


def propagate_kernel(me_ref, tile_hbm, grad_hbm, *refs):
    outs = refs[:-6]
    tile, grad, state, total, arrived, grad_arrived = refs[-6:]
    blocks = arrived.shape[0]
    replicas = len(outs)
    rows = tile.shape[0]
    depth = rows // blocks
    quarter = rows // replicas
    grad_copy = pltpu.make_async_copy(grad_hbm, grad, grad_arrived)
    grad_copy.start()
    copies = []
    for block in range(blocks):
        part = pl.ds(block * depth, depth)
        copies.append(
            pltpu.make_async_copy(tile_hbm.at[part], tile.at[part], arrived.at[block])
        )
        copies[-1].start()
    grad_copy.wait()
    first = grad[...].T
    state[...] = first
    for block in range(blocks):
        copies[block].wait()
        part = slice(block * depth, (block + 1) * depth)
        added = product(state[:, part], tile[part, :])
        if block == 0:
            total[...] = added
        else:
            total[...] += added
    second = total[...].astype(BF16)
    total[...] = first.astype(F32) + second.astype(F32)
    state[...] = second
    third = [
        product(state[...], tile[:, part * quarter : (part + 1) * quarter]).astype(BF16)
        for part in range(replicas)
    ]
    for part in range(replicas):
        state[:, part * quarter : (part + 1) * quarter] = third[part]
    for step in range(replicas):
        start = lax.rem(me_ref[0] + step, replicas) * quarter
        lanes = pl.ds(pl.multiple_of(start, quarter), quarter)
        last = product(state[...], tile[:, lanes]).astype(BF16)
        term = total[:, lanes] + state[:, lanes].astype(F32) + last.astype(F32)
        outs[step][...] = (term / F32(LAYERS + 1)).astype(BF16).T


def propagate(me, adjacency, start, replicas):
    rows, width = start.shape
    piece = shaped((rows // replicas, width), BF16)
    return call(
        propagate_kernel,
        [piece] * replicas,
        [SMEM, HBM, HBM],
        [VMEM] * replicas,
        scratch=[
            pltpu.VMEM((rows, rows), BF16),
            pltpu.VMEM((rows, width), BF16),
            pltpu.VMEM((width, rows), BF16),
            pltpu.VMEM((width, rows), F32),
            pltpu.SemaphoreType.DMA((BLOCKS,)),
            pltpu.SemaphoreType.DMA,
        ],
        mebi=60,
        flops=2 * LAYERS * rows * rows * width,
        moved=2 * rows * rows + 4 * rows * width,
    )(me, adjacency, start)


def plan_kernel(capacity, me_ref, owner_ref, slot_ref, pack_ref, unpack_ref, slots_ref):
    places, quarter = pack_ref.shape
    peers = places // capacity
    lanes = pl.ds(pl.multiple_of(me_ref[0] * quarter, quarter), quarter)
    owner = owner_ref[:, lanes]
    slot = slot_ref[:, lanes]
    hot = ids((peers, quarter), 0) == owner
    owner_hot = jnp.where(hot, 1.0, 0.0).astype(BF16)
    square = (quarter, quarter)
    upper = jnp.where(ids(square, 0) <= ids(square, 1), 1.0, 0.0).astype(BF16)
    running = product(owner_hot, upper)
    rank = jnp.sum(jnp.where(hot, running, 0.0), axis=0, keepdims=True).astype(jnp.int32) - 1
    place = owner * capacity + rank
    pack_ref[...] = jnp.where(ids(pack_ref.shape, 0) == place, 1.0, 0.0).astype(BF16)
    column = jnp.broadcast_to(place.astype(F32), (LANES, quarter)).T.astype(jnp.int32)
    for part in range(places // LANES):
        here = column == ids(column.shape, 1) + part * LANES
        unpack_ref[:, part * LANES : (part + 1) * LANES] = jnp.where(here, 1.0, 0.0).astype(BF16)
    index = ids((LANES, quarter), 0)
    digit = jnp.where(index < capacity, slot >> RADIX_BITS, slot & ((1 << RADIX_BITS) - 1))
    wanted = (index < 2 * capacity) & (lax.rem(index, capacity) == rank)
    spread = jnp.where(wanted, digit, 0).astype(F32).astype(BF16)
    lists = lax.dot_general(
        owner_hot, spread, (((1,), (1,)), ((), ())), preferred_element_type=F32
    )
    slots_ref[...] = lists.astype(BF16)


def plan(me, row_owner, table_slot, quarter, peers, capacity):
    rows = table_slot.shape[0]
    places = peers * capacity

    def kernel(*refs):
        plan_kernel(capacity, *refs)

    return call(
        kernel,
        [
            shaped((places, quarter), BF16),
            shaped((quarter, places), BF16),
            shaped((peers, LANES), BF16),
        ],
        [SMEM, VMEM, VMEM],
        [VMEM] * 3,
        flops=2 * quarter * quarter * peers,
        moved=4 * places * quarter,
    )(me, row_owner.reshape(1, rows), table_slot.reshape(1, rows))


def pack_kernel(pack_ref, slots_ref, *refs):
    *terms, out_ref = refs
    row_grad = terms[0][...].astype(F32)
    for term in terms[1:]:
        row_grad = row_grad + term[...].astype(F32)
    peers, pairs = out_ref.shape[:2]
    packed = product(pack_ref[...], row_grad.astype(BF16)).astype(BF16)
    out_ref[:, : pairs - 1] = packed.reshape(peers, pairs - 1, 2, LANES)
    lists = slots_ref[...]
    out_ref[:, pairs - 1] = jnp.broadcast_to(lists[:, None, :], (peers, 2, LANES))


def pack(matrix, slots, terms, capacity):
    peers = slots.shape[0]
    return call(
        pack_kernel,
        shaped((peers, capacity // 2 + 1, 2, LANES), BF16),
        [VMEM] * (2 + len(terms)),
        VMEM,
        flops=2 * matrix.shape[0] * matrix.shape[1] * LANES,
        moved=2 * matrix.shape[0] * (matrix.shape[1] + LANES),
    )(matrix, slots, *terms)


def accumulate_kernel(message_ref, partial_ref, receiver_ref):
    shard, places = receiver_ref.shape
    peers, pairs = message_ref.shape[:2]
    capacity = places // peers
    digits = message_ref[:, pairs - 1, 0, :]
    lane, place = ids((LANES, places), 0), ids((LANES, places), 1)
    rank = lax.rem(place, capacity)
    weight = jnp.where(
        lane == rank, float(1 << RADIX_BITS), jnp.where(lane == rank + capacity, 1.0, 0.0)
    ).astype(BF16)
    lists = product(digits, weight)
    mine = ids((peers, places), 0) == ids((peers, places), 1) // capacity
    slot = jnp.sum(jnp.where(mine, lists, 0.0), axis=0, keepdims=True).astype(jnp.int32)
    receiver_ref[...] = jnp.where(ids((shard, places), 0) == slot, 1.0, 0.0).astype(BF16)
    data = message_ref[:, : pairs - 1].reshape(places, LANES)
    partial_ref[...] = product(receiver_ref[...], data).astype(BF16)


def accumulate(message, shard, capacity):
    places = message.shape[0] * capacity
    return call(
        accumulate_kernel,
        [shaped((shard, LANES), BF16), shaped((shard, places), BF16)],
        [VMEM],
        [VMEM] * 2,
        flops=2 * shard * places * LANES,
        moved=2 * places * (shard + LANES),
    )(message)


def update_kernel(
    own_ref, across_ref, left_ref, right_ref, receiver_ref, table_ref, sums_ref,
    new_table_ref, new_sums_ref, answer_ref,
):
    grad = (own_ref[...].astype(F32) + across_ref[...].astype(F32)) + (
        left_ref[...].astype(F32) + right_ref[...].astype(F32)
    )
    mean = jnp.mean((grad * grad).T, axis=0, keepdims=True)
    sums = sums_ref[...] + mean
    new_sums_ref[...] = sums
    scale = jnp.broadcast_to(LEARN_RATE / jnp.sqrt(sums), (LANES, sums.shape[1])).T
    new_table = table_ref[...] - grad * scale
    new_table_ref[...] = new_table
    answer = product(new_table.T.astype(BF16), receiver_ref[...])
    answer_ref[...] = answer.T.astype(BF16)


def update(partials, receiver, table_rows, row_accumulators):
    shard, places = receiver.shape
    new_table, sums, answer = call(
        update_kernel,
        [shaped((shard, LANES), F32), shaped((1, shard), F32), shaped((places, LANES), BF16)],
        [VMEM] * 7,
        [VMEM] * 3,
        flops=2 * shard * places * LANES,
        moved=2 * places * (shard + LANES),
    )(*partials, receiver, table_rows, row_accumulators.reshape(1, shard))
    return new_table, sums.reshape(shard), answer


def unpack_kernel(matrix_ref, returned_ref, out_ref):
    out_ref[...] = product(matrix_ref[...], returned_ref[...]).astype(BF16)


def unpack(matrix, returned):
    quarter, places = matrix.shape
    return call(
        unpack_kernel,
        shaped((quarter, LANES), BF16),
        [VMEM] * 2,
        VMEM,
        flops=2 * quarter * places * LANES,
        moved=2 * places * (quarter + LANES),
    )(matrix, returned)


def place_kernel(steps, replicas, me_ref, *refs):
    pieces = refs[: len(steps)]
    out_hbm, sent = refs[-2:]
    quarter = pieces[0].shape[0]
    copies = []
    for index, step in enumerate(steps):
        source = lax.rem(me_ref[0] + replicas - step, replicas) * quarter
        rows = pl.ds(pl.multiple_of(source, quarter), quarter)
        copies.append(pltpu.make_async_copy(pieces[index], out_hbm.at[rows], sent.at[index]))
        copies[-1].start()
    for copy in copies:
        copy.wait()


def place(me, steps, pieces, replicas, rows, before=None):
    def kernel(*refs):
        place_kernel(steps, replicas, *refs)

    earlier = [] if before is None else [before]
    quarter, width = pieces[0].shape
    return pl.pallas_call(
        kernel,
        out_shape=shaped((rows, width), BF16),
        in_specs=[SMEM] + [VMEM] * len(pieces) + [HBM] * len(earlier),
        out_specs=HBM,
        scratch_shapes=[pltpu.SemaphoreType.DMA((len(pieces),))],
        input_output_aliases={1 + len(pieces): 0} if earlier else {},
        cost_estimate=pl.CostEstimate(
            flops=0, bytes_accessed=4 * quarter * width * len(pieces), transcendentals=0
        ),
    )(me, *pieces, *earlier)


def send(piece, step, replicas):
    return lax.ppermute(piece, "rep", [(i, (i + step) % replicas) for i in range(replicas)])


def send_order(replicas):
    return sorted(range(1, replicas), key=lambda step: -min(step, replicas - step))


def on_device(adjacency, grad_out, row_owner, table_slot, table_rows, row_accumulators):
    peers = lax.axis_size("dom")
    replicas = lax.axis_size("rep")
    rows = adjacency.shape[0]
    width = grad_out.shape[2]
    shard = table_rows.shape[0]
    quarter = rows // replicas
    capacity = max(2, 2 * quarter // peers)
    order = send_order(replicas)
    me = jnp.full((1,), lax.axis_index("rep"), jnp.int32)

    terms = propagate(me, adjacency, grad_out[0], replicas)
    got_terms = [send(terms[step], step, replicas) for step in order]
    later, _ = lax.optimization_barrier((me, terms[0]))
    to_places, from_places, slots = plan(later, row_owner, table_slot, quarter, peers, capacity)
    message = pack(to_places, slots, [terms[0], *got_terms], capacity)

    incoming = lax.all_to_all(message, "dom", split_axis=0, concat_axis=0, tiled=True)
    partial, receiver = accumulate(incoming, shard, capacity)
    partials = [partial] + [send(partial, step, replicas) for step in order]
    new_table, new_accumulators, answer = update(
        partials, receiver, table_rows, row_accumulators
    )

    returned = lax.all_to_all(
        answer.reshape(peers, capacity, width), "dom", split_axis=0, concat_axis=0, tiled=True
    )
    fresh = unpack(from_places, returned.reshape(peers * capacity, width))
    pieces = [send(fresh, step, replicas) for step in order]
    fresh_rows = place(me, [0, *order[:-1]], [fresh, *pieces[:-1]], replicas, rows)
    fresh_rows = place(me, order[-1:], pieces[-1:], replicas, rows, before=fresh_rows)
    return (new_table, new_accumulators, fresh_rows)


def solution(mesh):
    return jax.shard_map(
        on_device,
        mesh=mesh,
        in_specs=(
            P("dom", None),
            P("rep", "dom", None),
            P("dom", None),
            P("dom"),
            P("dom", None),
            P("dom"),
        ),
        out_specs=(P("dom", None), P("dom"), P("dom", None)),
        check_vma=False,
    )
```

```python
import jax
import jax.numpy as jnp
from jax import lax
from jax.experimental import pallas as pl
from jax.experimental.pallas import tpu as pltpu
from jax.sharding import PartitionSpec as P

LAYERS = 3
LEARN_RATE = 0.5
LANES = 128
BLOCKS = 8
RADIX_BITS = 4
MEBI = 1024 * 1024

VMEM = pl.BlockSpec(memory_space=pltpu.VMEM)
HBM = pl.BlockSpec(memory_space=pltpu.HBM)
BF16 = jnp.bfloat16
F32 = jnp.float32


def ids(shape, axis):
    return lax.broadcasted_iota(jnp.int32, shape, axis)


def product(left, right):
    return jnp.dot(left, right, preferred_element_type=F32)


def shaped(shape, dtype):
    return jax.ShapeDtypeStruct(shape, dtype)


def call(kernel, out_shape, in_specs, out_specs, scratch=(), mebi=16, flops=0, moved=0):
    return pl.pallas_call(
        kernel,
        out_shape=out_shape,
        in_specs=in_specs,
        out_specs=out_specs,
        scratch_shapes=list(scratch),
        compiler_params=pltpu.CompilerParams(vmem_limit_bytes=mebi * MEBI),
        cost_estimate=pl.CostEstimate(flops=flops, bytes_accessed=moved, transcendentals=0),
    )


def propagate_kernel(tile_hbm, grad_hbm, *refs):
    outs = refs[:-6]
    tile, grad, state, total, arrived, grad_arrived = refs[-6:]
    blocks = arrived.shape[0]
    replicas = len(outs)
    rows = tile.shape[0]
    depth = rows // blocks
    quarter = rows // replicas
    grad_copy = pltpu.make_async_copy(grad_hbm, grad, grad_arrived)
    grad_copy.start()
    copies = []
    for block in range(blocks):
        part = pl.ds(block * depth, depth)
        copies.append(
            pltpu.make_async_copy(tile_hbm.at[part], tile.at[part], arrived.at[block])
        )
        copies[-1].start()
    grad_copy.wait()
    first = grad[...].T
    state[...] = first
    for block in range(blocks):
        copies[block].wait()
        part = slice(block * depth, (block + 1) * depth)
        added = product(state[:, part], tile[part, :])
        if block == 0:
            total[...] = added
        else:
            total[...] += added
    second = total[...].astype(BF16)
    total[...] = first.astype(F32) + second.astype(F32)
    state[...] = second
    third = [
        product(state[...], tile[:, part * quarter : (part + 1) * quarter]).astype(BF16)
        for part in range(replicas)
    ]
    for part in range(replicas):
        state[:, part * quarter : (part + 1) * quarter] = third[part]
    for step in range(replicas):
        start = lax.rem(lax.axis_index("rep") + step, replicas) * quarter
        lanes = pl.ds(pl.multiple_of(start, quarter), quarter)
        last = product(state[...], tile[:, lanes]).astype(BF16)
        term = total[:, lanes] + state[:, lanes].astype(F32) + last.astype(F32)
        outs[step][...] = (term / F32(LAYERS + 1)).astype(BF16).T


def propagate(adjacency, start, replicas):
    rows, width = start.shape
    piece = shaped((rows // replicas, width), BF16)
    return call(
        propagate_kernel,
        [piece] * replicas,
        [HBM, HBM],
        [VMEM] * replicas,
        scratch=[
            pltpu.VMEM((rows, rows), BF16),
            pltpu.VMEM((rows, width), BF16),
            pltpu.VMEM((width, rows), BF16),
            pltpu.VMEM((width, rows), F32),
            pltpu.SemaphoreType.DMA((BLOCKS,)),
            pltpu.SemaphoreType.DMA,
        ],
        mebi=50,
        flops=2 * LAYERS * rows * rows * width,
        moved=2 * rows * rows + 4 * rows * width,
    )(adjacency, start)


def plan_kernel(capacity, owner_ref, slot_ref, pack_ref, unpack_ref, slots_ref):
    places, quarter = pack_ref.shape
    peers = places // capacity
    lanes = pl.ds(pl.multiple_of(lax.axis_index("rep") * quarter, quarter), quarter)
    owner = owner_ref[:, lanes]
    slot = slot_ref[:, lanes]
    hot = ids((peers, quarter), 0) == owner
    owner_hot = jnp.where(hot, 1.0, 0.0).astype(BF16)
    square = (quarter, quarter)
    upper = jnp.where(ids(square, 0) <= ids(square, 1), 1.0, 0.0).astype(BF16)
    running = product(owner_hot, upper)
    rank = jnp.sum(jnp.where(hot, running, 0.0), axis=0, keepdims=True).astype(jnp.int32) - 1
    place = owner * capacity + rank
    pack_ref[...] = jnp.where(ids(pack_ref.shape, 0) == place, 1.0, 0.0).astype(BF16)
    column = jnp.broadcast_to(place.astype(F32), (LANES, quarter)).T.astype(jnp.int32)
    for part in range(places // LANES):
        here = column == ids(column.shape, 1) + part * LANES
        unpack_ref[:, part * LANES : (part + 1) * LANES] = jnp.where(here, 1.0, 0.0).astype(BF16)
    index = ids((LANES, quarter), 0)
    digit = jnp.where(index < capacity, slot >> RADIX_BITS, slot & ((1 << RADIX_BITS) - 1))
    wanted = (index < 2 * capacity) & (lax.rem(index, capacity) == rank)
    spread = jnp.where(wanted, digit, 0).astype(F32).astype(BF16)
    lists = lax.dot_general(
        owner_hot, spread, (((1,), (1,)), ((), ())), preferred_element_type=F32
    )
    slots_ref[...] = lists.astype(BF16)


def plan(row_owner, table_slot, quarter, peers, capacity):
    rows = table_slot.shape[0]
    places = peers * capacity

    def kernel(*refs):
        plan_kernel(capacity, *refs)

    return call(
        kernel,
        [
            shaped((places, quarter), BF16),
            shaped((quarter, places), BF16),
            shaped((peers, LANES), BF16),
        ],
        [VMEM, VMEM],
        [VMEM] * 3,
        flops=2 * quarter * quarter * peers,
        moved=4 * places * quarter,
    )(row_owner.reshape(1, rows), table_slot.reshape(1, rows))


def pack_kernel(pack_ref, slots_ref, *refs):
    *terms, out_ref = refs
    row_grad = terms[0][...].astype(F32)
    for term in terms[1:]:
        row_grad = row_grad + term[...].astype(F32)
    peers, pairs = out_ref.shape[:2]
    packed = product(pack_ref[...], row_grad.astype(BF16)).astype(BF16)
    out_ref[:, : pairs - 1] = packed.reshape(peers, pairs - 1, 2, LANES)
    lists = slots_ref[...]
    out_ref[:, pairs - 1] = jnp.broadcast_to(lists[:, None, :], (peers, 2, LANES))


def pack(matrix, slots, terms, capacity):
    peers = slots.shape[0]
    return call(
        pack_kernel,
        shaped((peers, capacity // 2 + 1, 2, LANES), BF16),
        [VMEM] * (2 + len(terms)),
        VMEM,
        flops=2 * matrix.shape[0] * matrix.shape[1] * LANES,
        moved=2 * matrix.shape[0] * (matrix.shape[1] + LANES),
    )(matrix, slots, *terms)


def accumulate_kernel(message_ref, partial_ref, receiver_ref):
    shard, places = receiver_ref.shape
    peers, pairs = message_ref.shape[:2]
    capacity = places // peers
    digits = message_ref[:, pairs - 1, 0, :]
    lane, place = ids((LANES, places), 0), ids((LANES, places), 1)
    rank = lax.rem(place, capacity)
    weight = jnp.where(
        lane == rank, float(1 << RADIX_BITS), jnp.where(lane == rank + capacity, 1.0, 0.0)
    ).astype(BF16)
    lists = product(digits, weight)
    mine = ids((peers, places), 0) == ids((peers, places), 1) // capacity
    slot = jnp.sum(jnp.where(mine, lists, 0.0), axis=0, keepdims=True).astype(jnp.int32)
    receiver_ref[...] = jnp.where(ids((shard, places), 0) == slot, 1.0, 0.0).astype(BF16)
    data = message_ref[:, : pairs - 1].reshape(places, LANES)
    partial_ref[...] = product(receiver_ref[...], data).astype(BF16)


def accumulate(message, shard, capacity):
    places = message.shape[0] * capacity
    return call(
        accumulate_kernel,
        [shaped((shard, LANES), BF16), shaped((shard, places), BF16)],
        [VMEM],
        [VMEM] * 2,
        flops=2 * shard * places * LANES,
        moved=2 * places * (shard + LANES),
    )(message)


def update_kernel(
    own_ref, across_ref, left_ref, right_ref, receiver_ref, table_ref, sums_ref,
    new_table_ref, new_sums_ref, answer_ref,
):
    grad = (own_ref[...].astype(F32) + across_ref[...].astype(F32)) + (
        left_ref[...].astype(F32) + right_ref[...].astype(F32)
    )
    mean = jnp.mean((grad * grad).T, axis=0, keepdims=True)
    sums = sums_ref[...] + mean
    new_sums_ref[...] = sums
    scale = jnp.broadcast_to(LEARN_RATE / jnp.sqrt(sums), (LANES, sums.shape[1])).T
    new_table = table_ref[...] - grad * scale
    new_table_ref[...] = new_table
    answer = product(new_table.T.astype(BF16), receiver_ref[...])
    answer_ref[...] = answer.T.astype(BF16)


def update(partials, receiver, table_rows, row_accumulators):
    shard, places = receiver.shape
    new_table, sums, answer = call(
        update_kernel,
        [shaped((shard, LANES), F32), shaped((1, shard), F32), shaped((places, LANES), BF16)],
        [VMEM] * 7,
        [VMEM] * 3,
        flops=2 * shard * places * LANES,
        moved=2 * places * (shard + LANES),
    )(*partials, receiver, table_rows, row_accumulators.reshape(1, shard))
    return new_table, sums.reshape(shard), answer


def unpack_kernel(matrix_ref, returned_ref, out_ref):
    out_ref[...] = product(matrix_ref[...], returned_ref[...]).astype(BF16)


def unpack(matrix, returned):
    quarter, places = matrix.shape
    return call(
        unpack_kernel,
        shaped((quarter, LANES), BF16),
        [VMEM] * 2,
        VMEM,
        flops=2 * quarter * places * LANES,
        moved=2 * places * (quarter + LANES),
    )(matrix, returned)


def send(piece, step, replicas):
    return lax.ppermute(piece, "rep", [(i, (i + step) % replicas) for i in range(replicas)])


def send_order(replicas):
    return sorted(range(1, replicas), key=lambda step: -min(step, replicas - step))


def on_device(adjacency, grad_out, row_owner, table_slot, table_rows, row_accumulators):
    peers = lax.axis_size("dom")
    replicas = lax.axis_size("rep")
    rows = adjacency.shape[0]
    width = grad_out.shape[2]
    shard = table_rows.shape[0]
    quarter = rows // replicas
    capacity = max(2, 2 * quarter // peers)
    order = send_order(replicas)
    me = lax.axis_index("rep")

    terms = propagate(adjacency, grad_out[0], replicas)
    got_terms = [send(terms[step], step, replicas) for step in order]
    owners, _ = lax.optimization_barrier((row_owner, terms[0]))
    to_places, from_places, slots = plan(owners, table_slot, quarter, peers, capacity)
    message = pack(to_places, slots, [terms[0], *got_terms], capacity)

    incoming = lax.all_to_all(message, "dom", split_axis=0, concat_axis=0, tiled=True)
    partial, receiver = accumulate(incoming, shard, capacity)
    partials = [partial] + [send(partial, step, replicas) for step in order]
    new_table, new_accumulators, answer = update(
        partials, receiver, table_rows, row_accumulators
    )

    returned = lax.all_to_all(
        answer.reshape(peers, capacity, width), "dom", split_axis=0, concat_axis=0, tiled=True
    )
    fresh = unpack(from_places, returned.reshape(peers * capacity, width))
    pieces = [send(fresh, step, replicas) for step in order]
    fresh_rows = jnp.zeros((rows, width), BF16)
    for step, piece in zip([0, *order], [fresh, *pieces]):
        source = lax.rem(me + replicas - step, replicas) * quarter
        fresh_rows = lax.dynamic_update_slice(fresh_rows, piece, (source, 0))
    return (new_table, new_accumulators, fresh_rows)


def solution(mesh):
    return jax.shard_map(
        on_device,
        mesh=mesh,
        in_specs=(
            P("dom", None),
            P("rep", "dom", None),
            P("dom", None),
            P("dom"),
            P("dom", None),
            P("dom"),
        ),
        out_specs=(P("dom", None), P("dom"), P("dom", None)),
        check_vma=False,
    )
```

```python
import jax
import jax.numpy as jnp
from jax import lax
from jax.experimental import pallas as pl
from jax.experimental.pallas import tpu as pltpu
from jax.sharding import PartitionSpec as P

LAYERS = 3
LEARN_RATE = 0.5
LANES = 128
SUBLANES = 8
PACKED = 16
CHUNKS = 4
RADIX_BITS = 4
MEBI = 1024 * 1024

VMEM = pl.BlockSpec(memory_space=pltpu.VMEM)
HBM = pl.BlockSpec(memory_space=pltpu.HBM)
BF16 = jnp.bfloat16
F32 = jnp.float32


def ids(shape, axis):
    return lax.broadcasted_iota(jnp.int32, shape, axis)


def product(left, right):
    return jnp.dot(left, right, preferred_element_type=F32)


def shaped(shape, dtype):
    return jax.ShapeDtypeStruct(shape, dtype)


def call(kernel, out_shape, in_specs, out_specs, scratch=(), mebi=16, flops=0, moved=0):
    return pl.pallas_call(
        kernel,
        out_shape=out_shape,
        in_specs=in_specs,
        out_specs=out_specs,
        scratch_shapes=list(scratch),
        compiler_params=pltpu.CompilerParams(vmem_limit_bytes=mebi * MEBI),
        cost_estimate=pl.CostEstimate(flops=flops, bytes_accessed=moved, transcendentals=0),
    )


def split_kernel(grad_hbm, owner_hbm, slot_hbm, *refs):
    *pieces, owner, slot, grad, turned, arrived, lists_arrived = refs
    lists = [
        pltpu.make_async_copy(owner_hbm, owner, lists_arrived.at[0]),
        pltpu.make_async_copy(slot_hbm, slot, lists_arrived.at[1]),
    ]
    chunks = arrived.shape[0]
    depth = grad.shape[0] // chunks
    copies = []
    for chunk in range(chunks):
        part = pl.ds(chunk * depth, depth)
        copies.append(
            pltpu.make_async_copy(grad_hbm.at[part], grad.at[part], arrived.at[chunk])
        )
        copies[-1].start()
    for copy in lists:
        copy.start()
    for chunk in range(chunks):
        copies[chunk].wait()
        part = slice(chunk * depth, (chunk + 1) * depth)
        turned[:, part] = grad[part, :].T
    replicas, columns = len(pieces), pieces[0].shape[0]
    for step, piece in enumerate(pieces):
        start = lax.rem(lax.axis_index("rep") + step, replicas) * columns
        piece[...] = turned[pl.ds(pl.multiple_of(start, columns), columns), :]
    for copy in lists:
        copy.wait()


def split(grad, row_owner, table_slot, replicas):
    rows, width = grad.shape
    held = [grad, row_owner.reshape(1, rows), table_slot.reshape(1, rows)]
    *pieces, owner, slot = call(
        split_kernel,
        [shaped((width // replicas, rows), BF16)] * replicas
        + [pltpu.VMEM((1, rows), jnp.int32)] * 2,
        [HBM] * 3,
        [VMEM] * (replicas + 2),
        scratch=[
            pltpu.VMEM((rows, width), BF16),
            pltpu.VMEM((width, rows), BF16),
            pltpu.SemaphoreType.DMA((CHUNKS,)),
            pltpu.SemaphoreType.DMA((2,)),
        ],
    )(*[pltpu.with_memory_space_constraint(array, pltpu.HBM) for array in held])
    return pieces, owner, slot


def plan_kernel(
    capacity, tile_hbm, owner_ref, slot_ref, tile_ref, places_ref, slots_ref, weight_ref, mine_ref, arrived
):
    tile_copy = pltpu.make_async_copy(tile_hbm, tile_ref, arrived)
    tile_copy.start()
    quarters, quarter, places = places_ref.shape
    peers = places // capacity
    square = (quarter, quarter)
    upper = jnp.where(ids(square, 0) <= ids(square, 1), 1.0, 0.0).astype(BF16)
    index = ids((LANES, quarter), 0)
    lane = ids(mine_ref.shape, 0)
    lists = None
    for number in range(quarters):
        lanes = slice(number * quarter, (number + 1) * quarter)
        owner, slot = owner_ref[:, lanes], slot_ref[:, lanes]
        hot = ids((peers, quarter), 0) == owner
        owner_hot = jnp.where(hot, 1.0, 0.0).astype(BF16)
        running = product(owner_hot, upper)
        rank = jnp.sum(jnp.where(hot, running, 0.0), axis=0, keepdims=True).astype(jnp.int32) - 1
        place = (owner * capacity + rank).astype(F32)
        column = jnp.broadcast_to(place, (LANES, quarter)).T.astype(jnp.int32)
        for part in range(places // LANES):
            here = column == ids(column.shape, 1) + part * LANES
            places_ref[number, :, part * LANES : (part + 1) * LANES] = jnp.where(
                here, 1.0, 0.0
            ).astype(BF16)
        high, low = slot >> RADIX_BITS, slot & ((1 << RADIX_BITS) - 1)
        first = number * capacity + rank
        spread = jnp.where(
            index == first, high, jnp.where(index == first + quarters * capacity, low, 0)
        )
        added = lax.dot_general(
            owner_hot,
            spread.astype(F32).astype(BF16),
            (((1,), (1,)), ((), ())),
            preferred_element_type=F32,
        )
        lists = added if lists is None else lists + added
        lane, turn = ids((LANES, places), 0), lax.rem(ids((LANES, places), 1), capacity)
        turn = turn + number * capacity
        units = jnp.where(lane == turn + quarters * capacity, 1.0, 0.0)
        weight_ref[number] = jnp.where(lane == turn, float(1 << RADIX_BITS), units).astype(BF16)
    slots_ref[...] = lists.astype(BF16)
    mine = ids(mine_ref.shape, 0) == ids(mine_ref.shape, 1) // capacity
    mine_ref[...] = jnp.where(mine, 1.0, 0.0)
    tile_copy.wait()


def plan(adjacency, owner, slot, quarters, peers, capacity):
    rows = slot.shape[1]
    places = peers * capacity

    def kernel(*refs):
        plan_kernel(capacity, *refs)

    return call(
        kernel,
        [
            pltpu.VMEM(adjacency.shape, BF16),
            shaped((quarters, rows // quarters, places), BF16),
            shaped((peers, LANES), BF16),
            shaped((quarters, LANES, places), BF16),
            shaped((peers, places), F32),
        ],
        [HBM, VMEM, VMEM],
        [VMEM] * 5,
        scratch=[pltpu.SemaphoreType.DMA],
    )(pltpu.with_memory_space_constraint(adjacency, pltpu.HBM), owner, slot)


def propagate_kernel(*refs):
    *pieces, tile_ref, places_ref, slots_ref, out_ref = refs
    total = pieces[0][...].astype(F32)
    for piece in pieces[1:]:
        total = total + piece[...].astype(F32)
    state = total.astype(BF16)
    for _ in range(LAYERS):
        state = product(state, tile_ref[...]).astype(BF16)
        total = total + state.astype(F32)
    term = (total / F32(LAYERS + 1)).astype(BF16)
    quarters, quarter, _ = places_ref.shape
    packed = jnp.concatenate(
        [
            product(term[:, number * quarter : (number + 1) * quarter], places_ref[number])
            for number in range(quarters)
        ],
        axis=0,
    )
    peers, pairs = out_ref.shape[:2]
    out_ref[:, : pairs - 1] = packed.T.astype(BF16).reshape(peers, pairs - 1, 2, LANES)
    lists = slots_ref[...]
    out_ref[:, pairs - 1] = jnp.broadcast_to(lists[:, None, :], (peers, 2, LANES))


def propagate(pieces, tile, places, slots, capacity):
    peers = slots.shape[0]
    rows = tile.shape[0]
    return call(
        propagate_kernel,
        shaped((peers, capacity // 2 + 1, 2, LANES), BF16),
        [VMEM] * (len(pieces) + 3),
        VMEM,
        flops=2 * LAYERS * rows * rows * LANES,
        moved=2 * rows * rows,
    )(*pieces, tile, places, slots)


def accumulate_kernel(shard, message_ref, weight_ref, mine_ref, piece_ref, rows_ref):
    quarters, _, places = weight_ref.shape
    pairs = message_ref.shape[1]
    columns = LANES // quarters
    digits = message_ref[:, pairs - 1, 0, :]
    data = message_ref[:, : pairs - 1].reshape(places, LANES)
    block = ids((shard, LANES), 1) // columns
    index = ids((shard, places), 0).astype(jnp.int16)
    sums = None
    for number in range(quarters):
        lists = product(digits, weight_ref[number])
        slot = jnp.sum(lists * mine_ref[...], axis=0, keepdims=True).astype(jnp.int32)
        rows_ref[number] = jnp.broadcast_to(slot, rows_ref.shape[1:])
        wide = jnp.broadcast_to(slot, (PACKED, places)).astype(jnp.int16)
        hot = index == jnp.concatenate([wide] * (shard // PACKED), axis=0)
        receiver = jnp.where(hot, jnp.ones(hot.shape, BF16), jnp.zeros(hot.shape, BF16))
        added = product(receiver, data)
        sums = added if sums is None else jnp.where(block == number, added, sums)
    turned = sums.T
    whole = turned[:columns]
    for number in range(1, quarters):
        whole = whole + turned[number * columns : (number + 1) * columns]
    piece_ref[...] = whole.astype(BF16)


def accumulate(message, weight, mine, shard):
    quarters, _, places = weight.shape

    def kernel(*refs):
        accumulate_kernel(shard, *refs)

    return call(
        kernel,
        [
            shaped((LANES // quarters, shard), BF16),
            shaped((quarters, SUBLANES, places), jnp.int32),
        ],
        [VMEM] * 3,
        [VMEM] * 2,
        flops=2 * quarters * shard * places * LANES,
        moved=2 * places * (shard + LANES),
    )(message, weight, mine)


def prepare_kernel(rows_ref, sender_ref):
    places, shard = sender_ref.shape
    slot = rows_ref[lax.axis_index("rep")].astype(F32)
    column = jnp.concatenate([slot] * (LANES // SUBLANES), axis=0).T.astype(jnp.int32)
    for part in range(shard // LANES):
        here = column == ids(column.shape, 1) + part * LANES
        sender_ref[:, part * LANES : (part + 1) * LANES] = jnp.where(here, 1.0, 0.0).astype(BF16)


def prepare(rows, shard):
    places = rows.shape[2]
    return call(
        prepare_kernel, shaped((places, shard), BF16), [VMEM], VMEM, moved=2 * places * shard
    )(rows)


def update_kernel(steps, *refs):
    pieces = refs[: len(steps)]
    sender_ref, table_ref, sums_ref, new_table_ref, new_sums_ref, answer_ref, grad = refs[len(steps) :]
    replicas, columns = len(steps), pieces[0].shape[0]
    for step, piece in zip(steps, pieces):
        start = lax.rem(lax.axis_index("rep") + replicas - step, replicas) * columns
        grad[pl.ds(pl.multiple_of(start, columns), columns), :] = piece[...].astype(F32)
    whole = grad[...]
    sums = sums_ref[...] + jnp.mean(whole * whole, axis=0, keepdims=True)
    new_sums_ref[...] = sums
    step = whole * (LEARN_RATE * lax.rsqrt(sums))
    new_table = table_ref[...] - step.T
    new_table_ref[...] = new_table
    answer_ref[...] = product(sender_ref[...], new_table.astype(BF16)).astype(BF16)


def update(steps, pieces, sender, table_rows, row_accumulators):
    places, shard = sender.shape

    def kernel(*refs):
        update_kernel(steps, *refs)

    new_table, sums, answer = call(
        kernel,
        [shaped((shard, LANES), F32), shaped((1, shard), F32), shaped((places, LANES), BF16)],
        [VMEM] * (len(pieces) + 3),
        [VMEM] * 3,
        scratch=[pltpu.VMEM((LANES, shard), F32)],
        flops=2 * shard * places * LANES,
        moved=2 * places * (shard + LANES),
    )(*pieces, sender, table_rows, row_accumulators.reshape(1, shard))
    return new_table, sums.reshape(shard), answer


def unpack_kernel(places_ref, returned_ref, out_ref):
    matrix = places_ref[lax.axis_index("rep")]
    out_ref[...] = product(matrix, returned_ref[...]).astype(BF16)


def unpack(matrices, returned):
    _, quarter, places = matrices.shape
    return call(
        unpack_kernel,
        shaped((quarter, LANES), BF16),
        [VMEM] * 2,
        VMEM,
        flops=2 * quarter * places * LANES,
        moved=2 * places * (quarter + LANES),
    )(matrices, returned)


def send(piece, step, replicas):
    return lax.ppermute(piece, "rep", [(i, (i + step) % replicas) for i in range(replicas)])


def send_order(replicas):
    return sorted(range(1, replicas), key=lambda step: -min(step, replicas - step))


def on_device(adjacency, grad_out, row_owner, table_slot, table_rows, row_accumulators):
    peers = lax.axis_size("dom")
    replicas = lax.axis_size("rep")
    rows = adjacency.shape[0]
    width = grad_out.shape[2]
    shard = table_rows.shape[0]
    quarter = rows // replicas
    capacity = max(2, 2 * quarter // peers)
    order = send_order(replicas)
    me = lax.axis_index("rep")

    columns, owner, slot = split(grad_out[0], row_owner, table_slot, replicas)
    pieces = [columns[0]] + [send(columns[step], step, replicas) for step in order]
    tile, places, slots, weight, mine = plan(adjacency, owner, slot, replicas, peers, capacity)
    message = propagate(pieces, tile, places, slots, capacity)

    incoming = lax.all_to_all(message, "dom", split_axis=0, concat_axis=0, tiled=True)
    piece, lists = accumulate(incoming, weight, mine, shard)
    pieces = [piece] + [send(piece, step, replicas) for step in order]
    sender = prepare(lists, shard)
    new_table, new_accumulators, answer = update(
        [0, *order], pieces, sender, table_rows, row_accumulators
    )

    returned = lax.all_to_all(
        answer.reshape(peers, capacity, width), "dom", split_axis=0, concat_axis=0, tiled=True
    )
    fresh = unpack(places, returned.reshape(peers * capacity, width))
    pieces = [send(fresh, step, replicas) for step in order]
    fresh_rows = jnp.zeros((rows, width), BF16)
    for step, piece in zip([0, *order], [fresh, *pieces]):
        source = lax.rem(me + replicas - step, replicas) * quarter
        fresh_rows = lax.dynamic_update_slice(fresh_rows, piece, (source, 0))
    return (new_table, new_accumulators, fresh_rows)


def solution(mesh):
    return jax.shard_map(
        on_device,
        mesh=mesh,
        in_specs=(
            P("dom", None),
            P("rep", "dom", None),
            P("dom", None),
            P("dom"),
            P("dom", None),
            P("dom"),
        ),
        out_specs=(P("dom", None), P("dom"), P("dom", None)),
        check_vma=False,
    )
```

```python
import jax
import jax.numpy as jnp
from jax import lax
from jax.experimental import pallas as pl
from jax.experimental.pallas import tpu as pltpu
from jax.sharding import PartitionSpec as P

LAYERS = 3
LEARN_RATE = 0.5
LANES = 128
SUBLANES = 8
PACKED = 16
CHUNKS = 4
RADIX_BITS = 4
MEBI = 1024 * 1024

VMEM = pl.BlockSpec(memory_space=pltpu.VMEM)
HBM = pl.BlockSpec(memory_space=pltpu.HBM)
BF16 = jnp.bfloat16
F32 = jnp.float32


def ids(shape, axis):
    return lax.broadcasted_iota(jnp.int32, shape, axis)


def product(left, right):
    return jnp.dot(left, right, preferred_element_type=F32)


def shaped(shape, dtype):
    return jax.ShapeDtypeStruct(shape, dtype)


def call(kernel, out_shape, in_specs, out_specs, scratch=(), mebi=16, flops=0, moved=0):
    return pl.pallas_call(
        kernel,
        out_shape=out_shape,
        in_specs=in_specs,
        out_specs=out_specs,
        scratch_shapes=list(scratch),
        compiler_params=pltpu.CompilerParams(vmem_limit_bytes=mebi * MEBI),
        cost_estimate=pl.CostEstimate(flops=flops, bytes_accessed=moved, transcendentals=0),
    )


def split_kernel(grad_hbm, owner_hbm, slot_hbm, *refs):
    *pieces, owner, slot, grad, turned, arrived, lists_arrived = refs
    lists = [
        pltpu.make_async_copy(owner_hbm, owner, lists_arrived.at[0]),
        pltpu.make_async_copy(slot_hbm, slot, lists_arrived.at[1]),
    ]
    chunks = arrived.shape[0]
    depth = grad.shape[0] // chunks
    copies = []
    for chunk in range(chunks):
        part = pl.ds(chunk * depth, depth)
        copies.append(
            pltpu.make_async_copy(grad_hbm.at[part], grad.at[part], arrived.at[chunk])
        )
        copies[-1].start()
    for copy in lists:
        copy.start()
    for chunk in range(chunks):
        copies[chunk].wait()
        part = slice(chunk * depth, (chunk + 1) * depth)
        turned[:, part] = grad[part, :].T
    replicas, columns = len(pieces), pieces[0].shape[0]
    for step, piece in enumerate(pieces):
        start = lax.rem(lax.axis_index("rep") + step, replicas) * columns
        piece[...] = turned[pl.ds(pl.multiple_of(start, columns), columns), :]
    for copy in lists:
        copy.wait()


def split(grad, row_owner, table_slot, replicas):
    rows, width = grad.shape
    held = [grad, row_owner.reshape(1, rows), table_slot.reshape(1, rows)]
    *pieces, owner, slot = call(
        split_kernel,
        [shaped((width // replicas, rows), BF16)] * replicas
        + [pltpu.VMEM((1, rows), jnp.int32)] * 2,
        [HBM] * 3,
        [VMEM] * (replicas + 2),
        scratch=[
            pltpu.VMEM((rows, width), BF16),
            pltpu.VMEM((width, rows), BF16),
            pltpu.SemaphoreType.DMA((CHUNKS,)),
            pltpu.SemaphoreType.DMA((2,)),
        ],
    )(*[pltpu.with_memory_space_constraint(array, pltpu.HBM) for array in held])
    return pieces, owner, slot


def plan_kernel(
    capacity, tile_hbm, owner_ref, slot_ref, tile_ref, places_ref, slots_ref, weight_ref, mine_ref, arrived
):
    tile_copy = pltpu.make_async_copy(tile_hbm, tile_ref, arrived)
    tile_copy.start()
    quarters, quarter, places = places_ref.shape
    peers = places // capacity
    square = (quarter, quarter)
    upper = jnp.where(ids(square, 0) <= ids(square, 1), 1.0, 0.0).astype(BF16)
    index = ids((LANES, quarter), 0)
    lane = ids(mine_ref.shape, 0)
    lists = None
    for number in range(quarters):
        lanes = slice(number * quarter, (number + 1) * quarter)
        owner, slot = owner_ref[:, lanes], slot_ref[:, lanes]
        hot = ids((peers, quarter), 0) == owner
        owner_hot = jnp.where(hot, 1.0, 0.0).astype(BF16)
        running = product(owner_hot, upper)
        rank = jnp.sum(jnp.where(hot, running, 0.0), axis=0, keepdims=True).astype(jnp.int32) - 1
        place = (owner * capacity + rank).astype(F32)
        column = jnp.broadcast_to(place, (LANES, quarter)).T.astype(jnp.int32)
        for part in range(places // LANES):
            here = column == ids(column.shape, 1) + part * LANES
            places_ref[number, :, part * LANES : (part + 1) * LANES] = jnp.where(
                here, 1.0, 0.0
            ).astype(BF16)
        high, low = slot >> RADIX_BITS, slot & ((1 << RADIX_BITS) - 1)
        first = number * capacity + rank
        spread = jnp.where(
            index == first, high, jnp.where(index == first + quarters * capacity, low, 0)
        )
        added = lax.dot_general(
            owner_hot,
            spread.astype(F32).astype(BF16),
            (((1,), (1,)), ((), ())),
            preferred_element_type=F32,
        )
        lists = added if lists is None else lists + added
        lane, turn = ids((LANES, places), 0), lax.rem(ids((LANES, places), 1), capacity)
        turn = turn + number * capacity
        units = jnp.where(lane == turn + quarters * capacity, 1.0, 0.0)
        weight_ref[number] = jnp.where(lane == turn, float(1 << RADIX_BITS), units).astype(BF16)
    slots_ref[...] = lists.astype(BF16)
    mine = ids(mine_ref.shape, 0) == ids(mine_ref.shape, 1) // capacity
    mine_ref[...] = jnp.where(mine, 1.0, 0.0)
    tile_copy.wait()


def plan(adjacency, owner, slot, quarters, peers, capacity):
    rows = slot.shape[1]
    places = peers * capacity

    def kernel(*refs):
        plan_kernel(capacity, *refs)

    return call(
        kernel,
        [
            pltpu.VMEM(adjacency.shape, BF16),
            shaped((quarters, rows // quarters, places), BF16),
            shaped((peers, LANES), BF16),
            shaped((quarters, LANES, places), BF16),
            shaped((peers, places), F32),
        ],
        [HBM, VMEM, VMEM],
        [VMEM] * 5,
        scratch=[pltpu.SemaphoreType.DMA],
    )(pltpu.with_memory_space_constraint(adjacency, pltpu.HBM), owner, slot)


def propagate_kernel(*refs):
    *pieces, tile_ref, places_ref, slots_ref, out_ref = refs
    total = pieces[0][...].astype(F32)
    for piece in pieces[1:]:
        total = total + piece[...].astype(F32)
    state = total.astype(BF16)
    for _ in range(LAYERS):
        state = product(state, tile_ref[...]).astype(BF16)
        total = total + state.astype(F32)
    term = (total / F32(LAYERS + 1)).astype(BF16)
    quarters, quarter, _ = places_ref.shape
    packed = jnp.concatenate(
        [
            product(
                term[:, number * quarter : (number + 1) * quarter], places_ref[number]
            ).astype(BF16)
            for number in range(quarters)
        ],
        axis=0,
    )
    peers, pairs = out_ref.shape[:2]
    out_ref[:, : pairs - 1] = packed.T.reshape(peers, pairs - 1, 2, LANES)
    lists = slots_ref[...]
    out_ref[:, pairs - 1] = jnp.broadcast_to(lists[:, None, :], (peers, 2, LANES))


def propagate(pieces, tile, places, slots, capacity):
    peers = slots.shape[0]
    rows = tile.shape[0]
    return call(
        propagate_kernel,
        shaped((peers, capacity // 2 + 1, 2, LANES), BF16),
        [VMEM] * (len(pieces) + 3),
        VMEM,
        flops=2 * LAYERS * rows * rows * LANES,
        moved=2 * rows * rows,
    )(*pieces, tile, places, slots)


def accumulate_kernel(shard, message_ref, weight_ref, mine_ref, piece_ref, rows_ref):
    quarters, _, places = weight_ref.shape
    pairs = message_ref.shape[1]
    columns = LANES // quarters
    digits = message_ref[:, pairs - 1, 0, :]
    data = message_ref[:, : pairs - 1].reshape(places, LANES)
    block = ids((shard, LANES), 1) // columns
    index = ids((shard, places), 0).astype(jnp.int16)
    slots = []
    for number in range(quarters):
        lists = product(digits, weight_ref[number])
        slots.append(jnp.sum(lists * mine_ref[...], axis=0, keepdims=True).astype(jnp.int32))
        rows_ref[number] = jnp.broadcast_to(slots[number], rows_ref.shape[1:])
    sums = None
    for number in range(quarters):
        wide = jnp.broadcast_to(slots[number], (PACKED, places)).astype(jnp.int16)
        hot = index == jnp.concatenate([wide] * (shard // PACKED), axis=0)
        receiver = jnp.where(hot, jnp.ones(hot.shape, BF16), jnp.zeros(hot.shape, BF16))
        added = product(receiver, data)
        sums = added if sums is None else jnp.where(block == number, added, sums)
    turned = sums.T
    whole = turned[:columns]
    for number in range(1, quarters):
        whole = whole + turned[number * columns : (number + 1) * columns]
    piece_ref[...] = whole.astype(BF16)


def accumulate(message, weight, mine, shard):
    quarters, _, places = weight.shape

    def kernel(*refs):
        accumulate_kernel(shard, *refs)

    return call(
        kernel,
        [
            shaped((LANES // quarters, shard), BF16),
            shaped((quarters, SUBLANES, places), jnp.int32),
        ],
        [VMEM] * 3,
        [VMEM] * 2,
        flops=2 * quarters * shard * places * LANES,
        moved=2 * places * (shard + LANES),
    )(message, weight, mine)


def prepare_kernel(rows_ref, sender_ref):
    places, shard = sender_ref.shape
    slot = rows_ref[lax.axis_index("rep")].astype(F32)
    column = jnp.concatenate([slot] * (LANES // SUBLANES), axis=0).T.astype(jnp.int32)
    for part in range(shard // LANES):
        here = column == ids(column.shape, 1) + part * LANES
        sender_ref[:, part * LANES : (part + 1) * LANES] = jnp.where(here, 1.0, 0.0).astype(BF16)


def prepare(rows, shard):
    places = rows.shape[2]
    return call(
        prepare_kernel, shaped((places, shard), BF16), [VMEM], VMEM, moved=2 * places * shard
    )(rows)


def update_kernel(steps, *refs):
    pieces = refs[: len(steps)]
    sender_ref, table_ref, sums_ref, new_table_ref, new_sums_ref, answer_ref, grad = refs[len(steps) :]
    replicas, columns = len(steps), pieces[0].shape[0]
    for step, piece in zip(steps, pieces):
        start = lax.rem(lax.axis_index("rep") + replicas - step, replicas) * columns
        grad[pl.ds(pl.multiple_of(start, columns), columns), :] = piece[...].astype(F32)
    whole = grad[...]
    sums = sums_ref[...] + jnp.mean(whole * whole, axis=0, keepdims=True)
    new_sums_ref[...] = sums
    step = whole * (LEARN_RATE * lax.rsqrt(sums))
    new_table = table_ref[...] - step.T
    new_table_ref[...] = new_table
    answer_ref[...] = product(sender_ref[...], new_table.astype(BF16)).astype(BF16)


def update(steps, pieces, sender, table_rows, row_accumulators):
    places, shard = sender.shape

    def kernel(*refs):
        update_kernel(steps, *refs)

    new_table, sums, answer = call(
        kernel,
        [
            pltpu.VMEM((shard, LANES), F32),
            pltpu.VMEM((1, shard), F32),
            shaped((places, LANES), BF16),
        ],
        [VMEM] * (len(pieces) + 3),
        [VMEM] * 3,
        scratch=[pltpu.VMEM((LANES, shard), F32)],
        flops=2 * shard * places * LANES,
        moved=2 * places * (shard + LANES),
    )(*pieces, sender, table_rows, row_accumulators.reshape(1, shard))
    return new_table, sums.reshape(shard), answer


def unpack_kernel(places_ref, returned_ref, out_ref):
    matrix = places_ref[lax.axis_index("rep")]
    out_ref[...] = product(matrix, returned_ref[...]).astype(BF16)


def unpack(matrices, returned):
    _, quarter, places = matrices.shape
    return call(
        unpack_kernel,
        shaped((quarter, LANES), BF16),
        [VMEM] * 2,
        VMEM,
        flops=2 * quarter * places * LANES,
        moved=2 * places * (quarter + LANES),
    )(matrices, returned)


def send(piece, step, replicas):
    return lax.ppermute(piece, "rep", [(i, (i + step) % replicas) for i in range(replicas)])


def send_order(replicas):
    return sorted(range(1, replicas), key=lambda step: -min(step, replicas - step))


def on_device(adjacency, grad_out, row_owner, table_slot, table_rows, row_accumulators):
    peers = lax.axis_size("dom")
    replicas = lax.axis_size("rep")
    rows = adjacency.shape[0]
    width = grad_out.shape[2]
    shard = table_rows.shape[0]
    quarter = rows // replicas
    capacity = max(2, 2 * quarter // peers)
    order = send_order(replicas)
    me = lax.axis_index("rep")

    columns, owner, slot = split(grad_out[0], row_owner, table_slot, replicas)
    pieces = [columns[0]] + [send(columns[step], step, replicas) for step in order]
    tile, places, slots, weight, mine = plan(adjacency, owner, slot, replicas, peers, capacity)
    message = propagate(pieces, tile, places, slots, capacity)

    incoming = lax.all_to_all(message, "dom", split_axis=0, concat_axis=0, tiled=True)
    piece, lists = accumulate(incoming, weight, mine, shard)
    pieces = [piece] + [send(piece, step, replicas) for step in order]
    sender = prepare(lists, shard)
    new_table, new_accumulators, answer = update(
        [0, *order], pieces, sender, table_rows, row_accumulators
    )

    returned = lax.all_to_all(
        answer.reshape(peers, capacity, width), "dom", split_axis=0, concat_axis=0, tiled=True
    )
    fresh = unpack(places, returned.reshape(peers * capacity, width))
    pieces = [send(fresh, step, replicas) for step in order]
    fresh_rows = jnp.zeros((rows, width), BF16)
    for step, piece in zip([0, *order], [fresh, *pieces]):
        source = lax.rem(me + replicas - step, replicas) * quarter
        fresh_rows = lax.dynamic_update_slice(fresh_rows, piece, (source, 0))
    return (new_table, new_accumulators, fresh_rows)


def solution(mesh):
    return jax.shard_map(
        on_device,
        mesh=mesh,
        in_specs=(
            P("dom", None),
            P("rep", "dom", None),
            P("dom", None),
            P("dom"),
            P("dom", None),
            P("dom"),
        ),
        out_specs=(P("dom", None), P("dom"), P("dom", None)),
        check_vma=False,
    )
```

```python
import jax
import jax.numpy as jnp
from jax import lax
from jax.experimental import pallas as pl
from jax.experimental.pallas import tpu as pltpu
from jax.sharding import PartitionSpec as P

LAYERS = 3
LEARN_RATE = 0.5
LANES = 128
SUBLANES = 8
PACKED = 16
CHUNKS = 4
RADIX_BITS = 4
MEBI = 1024 * 1024

VMEM = pl.BlockSpec(memory_space=pltpu.VMEM)
HBM = pl.BlockSpec(memory_space=pltpu.HBM)
BF16 = jnp.bfloat16
F32 = jnp.float32


def ids(shape, axis):
    return lax.broadcasted_iota(jnp.int32, shape, axis)


def product(left, right):
    return jnp.dot(left, right, preferred_element_type=F32)


def shaped(shape, dtype):
    return jax.ShapeDtypeStruct(shape, dtype)


def call(kernel, out_shape, in_specs, out_specs, scratch=(), mebi=16, flops=0, moved=0):
    return pl.pallas_call(
        kernel,
        out_shape=out_shape,
        in_specs=in_specs,
        out_specs=out_specs,
        scratch_shapes=list(scratch),
        compiler_params=pltpu.CompilerParams(vmem_limit_bytes=mebi * MEBI),
        cost_estimate=pl.CostEstimate(flops=flops, bytes_accessed=moved, transcendentals=0),
    )


def split_kernel(grad_hbm, owner_hbm, slot_hbm, *refs):
    *pieces, owner, slot, grad, turned, arrived, lists_arrived = refs
    lists = [
        pltpu.make_async_copy(owner_hbm, owner, lists_arrived.at[0]),
        pltpu.make_async_copy(slot_hbm, slot, lists_arrived.at[1]),
    ]
    chunks = arrived.shape[0]
    depth = grad.shape[0] // chunks
    copies = []
    for chunk in range(chunks):
        part = pl.ds(chunk * depth, depth)
        copies.append(
            pltpu.make_async_copy(grad_hbm.at[part], grad.at[part], arrived.at[chunk])
        )
        copies[-1].start()
    for copy in lists:
        copy.start()
    for chunk in range(chunks):
        copies[chunk].wait()
        part = slice(chunk * depth, (chunk + 1) * depth)
        turned[:, part] = grad[part, :].T
    replicas, columns = len(pieces), pieces[0].shape[0]
    for step, piece in enumerate(pieces):
        start = lax.rem(lax.axis_index("rep") + step, replicas) * columns
        piece[...] = turned[pl.ds(pl.multiple_of(start, columns), columns), :]
    for copy in lists:
        copy.wait()


def split(grad, row_owner, table_slot, replicas):
    rows, width = grad.shape
    held = [grad, row_owner.reshape(1, rows), table_slot.reshape(1, rows)]
    *pieces, owner, slot = call(
        split_kernel,
        [shaped((width // replicas, rows), BF16)] * replicas
        + [pltpu.VMEM((1, rows), jnp.int32)] * 2,
        [HBM] * 3,
        [VMEM] * (replicas + 2),
        scratch=[
            pltpu.VMEM((rows, width), BF16),
            pltpu.VMEM((width, rows), BF16),
            pltpu.SemaphoreType.DMA((CHUNKS,)),
            pltpu.SemaphoreType.DMA((2,)),
        ],
    )(*[pltpu.with_memory_space_constraint(array, pltpu.HBM) for array in held])
    return pieces, owner, slot


def plan_kernel(
    capacity, tile_hbm, owner_ref, slot_ref, tile_ref, places_ref, slots_ref, weight_ref, mine_ref, arrived
):
    tile_copy = pltpu.make_async_copy(tile_hbm, tile_ref, arrived)
    tile_copy.start()
    quarters, quarter, places = places_ref.shape
    peers = places // capacity
    square = (quarter, quarter)
    upper = jnp.where(ids(square, 0) <= ids(square, 1), 1.0, 0.0).astype(BF16)
    index = ids((LANES, quarter), 0)
    lane = ids(mine_ref.shape, 0)
    lists = None
    for number in range(quarters):
        lanes = slice(number * quarter, (number + 1) * quarter)
        owner, slot = owner_ref[:, lanes], slot_ref[:, lanes]
        hot = ids((peers, quarter), 0) == owner
        owner_hot = jnp.where(hot, 1.0, 0.0).astype(BF16)
        running = product(owner_hot, upper)
        rank = jnp.sum(jnp.where(hot, running, 0.0), axis=0, keepdims=True).astype(jnp.int32) - 1
        place = (owner * capacity + rank).astype(F32)
        column = jnp.broadcast_to(place, (LANES, quarter)).T.astype(jnp.int32)
        for part in range(places // LANES):
            here = column == ids(column.shape, 1) + part * LANES
            places_ref[number, :, part * LANES : (part + 1) * LANES] = jnp.where(
                here, 1.0, 0.0
            ).astype(BF16)
        high, low = slot >> RADIX_BITS, slot & ((1 << RADIX_BITS) - 1)
        first = number * capacity + rank
        spread = jnp.where(
            index == first, high, jnp.where(index == first + quarters * capacity, low, 0)
        )
        added = lax.dot_general(
            owner_hot,
            spread.astype(F32).astype(BF16),
            (((1,), (1,)), ((), ())),
            preferred_element_type=F32,
        )
        lists = added if lists is None else lists + added
        lane, turn = ids((LANES, places), 0), lax.rem(ids((LANES, places), 1), capacity)
        turn = turn + number * capacity
        units = jnp.where(lane == turn + quarters * capacity, 1.0, 0.0)
        weight_ref[number] = jnp.where(lane == turn, float(1 << RADIX_BITS), units).astype(BF16)
    slots_ref[...] = lists.astype(BF16)
    mine = ids(mine_ref.shape, 0) == ids(mine_ref.shape, 1) // capacity
    mine_ref[...] = jnp.where(mine, 1.0, 0.0)
    tile_copy.wait()


def plan(adjacency, owner, slot, quarters, peers, capacity):
    rows = slot.shape[1]
    places = peers * capacity

    def kernel(*refs):
        plan_kernel(capacity, *refs)

    return call(
        kernel,
        [
            pltpu.VMEM(adjacency.shape, BF16),
            shaped((quarters, rows // quarters, places), BF16),
            shaped((peers, LANES), BF16),
            shaped((quarters, LANES, places), BF16),
            shaped((peers, places), F32),
        ],
        [HBM, VMEM, VMEM],
        [VMEM] * 5,
        scratch=[pltpu.SemaphoreType.DMA],
    )(pltpu.with_memory_space_constraint(adjacency, pltpu.HBM), owner, slot)


def propagate_kernel(*refs):
    *pieces, tile_ref, places_ref, slots_ref, out_ref = refs
    total = pieces[0][...].astype(F32)
    for piece in pieces[1:]:
        total = total + piece[...].astype(F32)
    state = total.astype(BF16)
    columns = state.shape[0]
    quarters, quarter, _ = places_ref.shape
    for _ in range(LAYERS):
        full = jnp.concatenate([state] * (LANES // columns), axis=0)
        state = product(full, tile_ref[...])[:columns].astype(BF16)
        total = total + state.astype(F32)
    term = (total / F32(LAYERS + 1)).astype(BF16)
    full = jnp.concatenate(
        [term[:, number * quarter : (number + 1) * quarter] for number in range(quarters)], axis=0
    )
    packed = jnp.concatenate(
        [
            product(full, places_ref[number])[number * columns : (number + 1) * columns].astype(BF16)
            for number in range(quarters)
        ],
        axis=0,
    )
    peers, pairs = out_ref.shape[:2]
    out_ref[:, : pairs - 1] = packed.T.reshape(peers, pairs - 1, 2, LANES)
    lists = slots_ref[...]
    out_ref[:, pairs - 1] = jnp.broadcast_to(lists[:, None, :], (peers, 2, LANES))


def propagate(pieces, tile, places, slots, capacity):
    peers = slots.shape[0]
    rows = tile.shape[0]
    return call(
        propagate_kernel,
        shaped((peers, capacity // 2 + 1, 2, LANES), BF16),
        [VMEM] * (len(pieces) + 3),
        VMEM,
        flops=2 * LAYERS * rows * rows * LANES,
        moved=2 * rows * rows,
    )(*pieces, tile, places, slots)


def accumulate_kernel(shard, message_ref, weight_ref, mine_ref, piece_ref, rows_ref):
    quarters, _, places = weight_ref.shape
    pairs = message_ref.shape[1]
    columns = LANES // quarters
    digits = message_ref[:, pairs - 1, 0, :]
    data = message_ref[:, : pairs - 1].reshape(places, LANES)
    block = ids((shard, LANES), 1) // columns
    index = ids((shard, places), 0).astype(jnp.int16)
    slots = []
    for number in range(quarters):
        lists = product(digits, weight_ref[number])
        slots.append(jnp.sum(lists * mine_ref[...], axis=0, keepdims=True).astype(jnp.int32))
        rows_ref[number] = jnp.broadcast_to(slots[number], rows_ref.shape[1:])
    sums = None
    for number in range(quarters):
        wide = jnp.broadcast_to(slots[number], (PACKED, places)).astype(jnp.int16)
        hot = index == jnp.concatenate([wide] * (shard // PACKED), axis=0)
        receiver = jnp.where(hot, jnp.ones(hot.shape, BF16), jnp.zeros(hot.shape, BF16))
        added = product(receiver, data)
        sums = added if sums is None else jnp.where(block == number, added, sums)
    turned = sums.T
    whole = turned[:columns]
    for number in range(1, quarters):
        whole = whole + turned[number * columns : (number + 1) * columns]
    piece_ref[...] = whole.astype(BF16)


def accumulate(message, weight, mine, shard):
    quarters, _, places = weight.shape

    def kernel(*refs):
        accumulate_kernel(shard, *refs)

    return call(
        kernel,
        [
            shaped((LANES // quarters, shard), BF16),
            shaped((quarters, SUBLANES, places), jnp.int32),
        ],
        [VMEM] * 3,
        [VMEM] * 2,
        flops=2 * quarters * shard * places * LANES,
        moved=2 * places * (shard + LANES),
    )(message, weight, mine)


def prepare_kernel(rows_ref, sender_ref):
    places, shard = sender_ref.shape
    slot = rows_ref[lax.axis_index("rep")].astype(F32)
    column = jnp.concatenate([slot] * (LANES // SUBLANES), axis=0).T.astype(jnp.int32)
    for part in range(shard // LANES):
        here = column == ids(column.shape, 1) + part * LANES
        sender_ref[:, part * LANES : (part + 1) * LANES] = jnp.where(here, 1.0, 0.0).astype(BF16)


def prepare(rows, shard):
    places = rows.shape[2]
    return call(
        prepare_kernel, shaped((places, shard), BF16), [VMEM], VMEM, moved=2 * places * shard
    )(rows)


def update_kernel(steps, *refs):
    pieces = refs[: len(steps)]
    sender_ref, table_ref, sums_ref, new_table_ref, new_sums_ref, answer_ref, grad = refs[len(steps) :]
    replicas, columns = len(steps), pieces[0].shape[0]
    for step, piece in zip(steps, pieces):
        start = lax.rem(lax.axis_index("rep") + replicas - step, replicas) * columns
        grad[pl.ds(pl.multiple_of(start, columns), columns), :] = piece[...].astype(F32)
    whole = grad[...]
    sums = sums_ref[...] + jnp.mean(whole * whole, axis=0, keepdims=True)
    new_sums_ref[...] = sums
    step = whole * (LEARN_RATE * lax.rsqrt(sums))
    new_table = table_ref[...] - step.T
    new_table_ref[...] = new_table
    answer_ref[...] = product(sender_ref[...], new_table.astype(BF16)).astype(BF16)


def update(steps, pieces, sender, table_rows, row_accumulators):
    places, shard = sender.shape

    def kernel(*refs):
        update_kernel(steps, *refs)

    new_table, sums, answer = call(
        kernel,
        [
            pltpu.VMEM((shard, LANES), F32),
            pltpu.VMEM((1, shard), F32),
            shaped((places, LANES), BF16),
        ],
        [VMEM] * (len(pieces) + 3),
        [VMEM] * 3,
        scratch=[pltpu.VMEM((LANES, shard), F32)],
        flops=2 * shard * places * LANES,
        moved=2 * places * (shard + LANES),
    )(*pieces, sender, table_rows, row_accumulators.reshape(1, shard))
    return new_table, sums.reshape(shard), answer


def unpack_kernel(places_ref, returned_ref, out_ref):
    matrix = places_ref[lax.axis_index("rep")]
    out_ref[...] = product(matrix, returned_ref[...]).astype(BF16)


def unpack(matrices, returned):
    _, quarter, places = matrices.shape
    return call(
        unpack_kernel,
        shaped((quarter, LANES), BF16),
        [VMEM] * 2,
        VMEM,
        flops=2 * quarter * places * LANES,
        moved=2 * places * (quarter + LANES),
    )(matrices, returned)


def send(piece, step, replicas):
    return lax.ppermute(piece, "rep", [(i, (i + step) % replicas) for i in range(replicas)])


def send_order(replicas):
    return sorted(range(1, replicas), key=lambda step: -min(step, replicas - step))


def on_device(adjacency, grad_out, row_owner, table_slot, table_rows, row_accumulators):
    peers = lax.axis_size("dom")
    replicas = lax.axis_size("rep")
    rows = adjacency.shape[0]
    width = grad_out.shape[2]
    shard = table_rows.shape[0]
    quarter = rows // replicas
    capacity = max(2, 2 * quarter // peers)
    order = send_order(replicas)
    me = lax.axis_index("rep")

    columns, owner, slot = split(grad_out[0], row_owner, table_slot, replicas)
    pieces = [columns[0]] + [send(columns[step], step, replicas) for step in order]
    tile, places, slots, weight, mine = plan(adjacency, owner, slot, replicas, peers, capacity)
    message = propagate(pieces, tile, places, slots, capacity)

    incoming = lax.all_to_all(message, "dom", split_axis=0, concat_axis=0, tiled=True)
    piece, lists = accumulate(incoming, weight, mine, shard)
    pieces = [piece] + [send(piece, step, replicas) for step in order]
    sender = prepare(lists, shard)
    new_table, new_accumulators, answer = update(
        [0, *order], pieces, sender, table_rows, row_accumulators
    )

    returned = lax.all_to_all(
        answer.reshape(peers, capacity, width), "dom", split_axis=0, concat_axis=0, tiled=True
    )
    fresh = unpack(places, returned.reshape(peers * capacity, width))
    pieces = [send(fresh, step, replicas) for step in order]
    fresh_rows = jnp.zeros((rows, width), BF16)
    for step, piece in zip([0, *order], [fresh, *pieces]):
        source = lax.rem(me + replicas - step, replicas) * quarter
        fresh_rows = lax.dynamic_update_slice(fresh_rows, piece, (source, 0))
    return (new_table, new_accumulators, fresh_rows)


def solution(mesh):
    return jax.shard_map(
        on_device,
        mesh=mesh,
        in_specs=(
            P("dom", None),
            P("rep", "dom", None),
            P("dom", None),
            P("dom"),
            P("dom", None),
            P("dom"),
        ),
        out_specs=(P("dom", None), P("dom"), P("dom", None)),
        check_vma=False,
    )
```

```python
import jax
import jax.numpy as jnp
from jax import lax
from jax.experimental import pallas as pl
from jax.experimental.pallas import tpu as pltpu
from jax.sharding import Mesh
from jax.sharding import PartitionSpec as P

LAYERS = 3
LEARN_RATE = 0.5
LANES = 128
SUBLANES = 8
PACKED = 16
CHUNKS = 4
CORES = 2
RADIX_BITS = 4
MEBI = 1024 * 1024

VMEM = pl.BlockSpec(memory_space=pltpu.VMEM)
HBM = pl.BlockSpec(memory_space=pltpu.HBM)
BF16 = jnp.bfloat16
F32 = jnp.float32


def ids(shape, axis):
    return lax.broadcasted_iota(jnp.int32, shape, axis)


def product(left, right):
    return jnp.dot(left, right, preferred_element_type=F32)


def shaped(shape, dtype):
    return jax.ShapeDtypeStruct(shape, dtype)


def call(kernel, out_shape, in_specs, out_specs, scratch=(), mebi=16, flops=0, moved=0):
    return pl.pallas_call(
        kernel,
        out_shape=out_shape,
        in_specs=in_specs,
        out_specs=out_specs,
        scratch_shapes=list(scratch),
        compiler_params=pltpu.CompilerParams(vmem_limit_bytes=mebi * MEBI),
        cost_estimate=pl.CostEstimate(flops=flops, bytes_accessed=moved, transcendentals=0),
    )


def split_kernel(grad_hbm, owner_hbm, slot_hbm, *refs):
    *pieces, owner, slot, grad, turned, arrived, lists_arrived = refs
    lists = [
        pltpu.make_async_copy(owner_hbm, owner, lists_arrived.at[0]),
        pltpu.make_async_copy(slot_hbm, slot, lists_arrived.at[1]),
    ]
    chunks = arrived.shape[0]
    depth = grad.shape[0] // chunks
    copies = []
    for chunk in range(chunks):
        part = pl.ds(chunk * depth, depth)
        copies.append(
            pltpu.make_async_copy(grad_hbm.at[part], grad.at[part], arrived.at[chunk])
        )
        copies[-1].start()
    for copy in lists:
        copy.start()
    for chunk in range(chunks):
        copies[chunk].wait()
        part = slice(chunk * depth, (chunk + 1) * depth)
        turned[:, part] = grad[part, :].T
    replicas, columns = len(pieces), pieces[0].shape[0]
    for step, piece in enumerate(pieces):
        start = lax.rem(lax.axis_index("rep") + step, replicas) * columns
        piece[...] = turned[pl.ds(pl.multiple_of(start, columns), columns), :]
    for copy in lists:
        copy.wait()


def split(grad, row_owner, table_slot, replicas):
    rows, width = grad.shape
    held = [grad, row_owner.reshape(1, rows), table_slot.reshape(1, rows)]
    *pieces, owner, slot = call(
        split_kernel,
        [shaped((width // replicas, rows), BF16)] * replicas
        + [pltpu.VMEM((1, rows), jnp.int32)] * 2,
        [HBM] * 3,
        [VMEM] * (replicas + 2),
        scratch=[
            pltpu.VMEM((rows, width), BF16),
            pltpu.VMEM((width, rows), BF16),
            pltpu.SemaphoreType.DMA((CHUNKS,)),
            pltpu.SemaphoreType.DMA((2,)),
        ],
    )(*[pltpu.with_memory_space_constraint(array, pltpu.HBM) for array in held])
    return pieces, owner, slot


def plan_kernel(
    capacity, cores, tile_hbm, owner_ref, slot_ref, tile_ref, places_ref, slots_ref, weight_ref, mine_ref, arrived
):
    tile_copy = pltpu.make_async_copy(tile_hbm, tile_ref, arrived)
    tile_copy.start()
    quarters, quarter, places = places_ref.shape
    peers = places // capacity
    square = (quarter, quarter)
    upper = jnp.where(ids(square, 0) <= ids(square, 1), 1.0, 0.0).astype(BF16)
    index = ids((LANES, quarter), 0)
    lane = ids(mine_ref.shape, 0)
    lists = None
    for number in range(quarters):
        lanes = slice(number * quarter, (number + 1) * quarter)
        named, slot = owner_ref[:, lanes], slot_ref[:, lanes]
        other = lax.rem(named + lax.axis_index("core"), cores)
        owner = other * (peers // cores) + lax.div(named, cores)
        hot = ids((peers, quarter), 0) == owner
        owner_hot = jnp.where(hot, 1.0, 0.0).astype(BF16)
        running = product(owner_hot, upper)
        rank = jnp.sum(jnp.where(hot, running, 0.0), axis=0, keepdims=True).astype(jnp.int32) - 1
        place = (owner * capacity + rank).astype(F32)
        column = jnp.broadcast_to(place, (LANES, quarter)).T.astype(jnp.int32)
        for part in range(places // LANES):
            here = column == ids(column.shape, 1) + part * LANES
            places_ref[number, :, part * LANES : (part + 1) * LANES] = jnp.where(
                here, 1.0, 0.0
            ).astype(BF16)
        high, low = slot >> RADIX_BITS, slot & ((1 << RADIX_BITS) - 1)
        first = number * capacity + rank
        spread = jnp.where(
            index == first, high, jnp.where(index == first + quarters * capacity, low, 0)
        )
        added = lax.dot_general(
            owner_hot,
            spread.astype(F32).astype(BF16),
            (((1,), (1,)), ((), ())),
            preferred_element_type=F32,
        )
        lists = added if lists is None else lists + added
        shape = weight_ref.shape[1:]
        lane, turn = ids(shape, 0), lax.rem(ids(shape, 1), capacity)
        turn = turn + number * capacity
        units = jnp.where(lane == turn + quarters * capacity, 1.0, 0.0)
        weight_ref[number] = jnp.where(lane == turn, float(1 << RADIX_BITS), units).astype(BF16)
    slots_ref[...] = lists.astype(BF16)
    mine = ids(mine_ref.shape, 0) == ids(mine_ref.shape, 1) // capacity
    mine_ref[...] = jnp.where(mine, 1.0, 0.0)
    tile_copy.wait()


def plan(adjacency, owner, slot, quarters, peers, cores, capacity):
    rows = slot.shape[1]
    places = peers * capacity

    def kernel(*refs):
        plan_kernel(capacity, cores, *refs)

    return call(
        kernel,
        [
            pltpu.VMEM(adjacency.shape, BF16),
            shaped((quarters, rows // quarters, places), BF16),
            shaped((peers, LANES), BF16),
            shaped((quarters, LANES, places // cores), BF16),
            shaped((peers // cores, places // cores), F32),
        ],
        [HBM, VMEM, VMEM],
        [VMEM] * 5,
        scratch=[pltpu.SemaphoreType.DMA],
    )(pltpu.with_memory_space_constraint(adjacency, pltpu.HBM), owner, slot)


def propagate_kernel(*refs):
    *pieces, tile_ref, places_ref, slots_ref, out_ref = refs
    total = pieces[0][...].astype(F32)
    for piece in pieces[1:]:
        total = total + piece[...].astype(F32)
    state = total.astype(BF16)
    columns = state.shape[0]
    quarters, quarter, _ = places_ref.shape
    for _ in range(LAYERS):
        full = jnp.concatenate([state] * (LANES // columns), axis=0)
        state = product(full, tile_ref[...])[:columns].astype(BF16)
        total = total + state.astype(F32)
    term = (total / F32(LAYERS + 1)).astype(BF16)
    full = jnp.concatenate(
        [term[:, number * quarter : (number + 1) * quarter] for number in range(quarters)], axis=0
    )
    packed = jnp.concatenate(
        [
            product(full, places_ref[number])[number * columns : (number + 1) * columns].astype(BF16)
            for number in range(quarters)
        ],
        axis=0,
    )
    chips, cores, pairs = out_ref.shape[:3]
    packed = packed.T.reshape(cores, chips, pairs - 1, 2, LANES)
    lists = slots_ref[...]
    for core in range(cores):
        out_ref[:, core, : pairs - 1] = packed[core]
        own = lists[core * chips : (core + 1) * chips]
        out_ref[:, core, pairs - 1] = jnp.broadcast_to(own[:, None, :], (chips, 2, LANES))


def propagate(pieces, tile, places, slots, cores, capacity):
    chips = slots.shape[0] // cores
    rows = tile.shape[0]
    return call(
        propagate_kernel,
        shaped((chips, cores, capacity // 2 + 1, 2, LANES), BF16),
        [VMEM] * (len(pieces) + 3),
        VMEM,
        flops=2 * LAYERS * rows * rows * LANES,
        moved=2 * rows * rows,
    )(*pieces, tile, places, slots)


def accumulate_kernel(shard, message_ref, weight_ref, mine_ref, *refs):
    *before, piece_ref, rows_ref = refs
    quarters, _, places = weight_ref.shape
    message = message_ref.at[:, 0]
    pairs = message.shape[1]
    columns = LANES // quarters
    digits = message[:, pairs - 1, 0, :]
    data = message[:, : pairs - 1].reshape(places, LANES)
    block = ids((shard, LANES), 1) // columns
    index = ids((shard, places), 0).astype(jnp.int16)
    slots = []
    for number in range(quarters):
        lists = product(digits, weight_ref[number])
        slots.append(jnp.sum(lists * mine_ref[...], axis=0, keepdims=True).astype(jnp.int32))
        rows_ref[number] = jnp.broadcast_to(slots[number], rows_ref.shape[1:])
    sums = None
    for number in range(quarters):
        wide = jnp.broadcast_to(slots[number], (PACKED, places)).astype(jnp.int16)
        hot = index == jnp.concatenate([wide] * (shard // PACKED), axis=0)
        receiver = jnp.where(hot, jnp.ones(hot.shape, BF16), jnp.zeros(hot.shape, BF16))
        added = product(receiver, data)
        sums = added if sums is None else jnp.where(block == number, added, sums)
    if before:
        piece = before[0][...] + sums
        turned = piece.T
        whole = turned[:columns]
        for number in range(1, quarters):
            whole = whole + turned[number * columns : (number + 1) * columns]
        piece_ref[...] = whole.astype(BF16)
    else:
        piece_ref[...] = sums


def accumulate(message, weight, mine, shard, before=None):
    quarters, _, places = weight.shape

    def kernel(*refs):
        accumulate_kernel(shard, *refs)

    piece = shaped((shard, LANES), F32)
    if before is not None:
        piece = shaped((LANES // quarters, shard), BF16)
    earlier = [] if before is None else [before]
    return call(
        kernel,
        [piece, shaped((quarters, SUBLANES, places), jnp.int32)],
        [VMEM] * (3 + len(earlier)),
        [VMEM] * 2,
        flops=2 * quarters * shard * places * LANES,
        moved=2 * places * (shard + LANES),
    )(message, weight, mine, *earlier)


def prepare_kernel(same_ref, other_ref, sender_ref):
    places, shard = sender_ref.shape
    me = lax.axis_index("rep")
    slot = jnp.concatenate([same_ref[me], other_ref[me]], axis=1).astype(F32)
    column = jnp.concatenate([slot] * (LANES // SUBLANES), axis=0).T.astype(jnp.int32)
    for part in range(shard // LANES):
        here = column == ids(column.shape, 1) + part * LANES
        sender_ref[:, part * LANES : (part + 1) * LANES] = jnp.where(here, 1.0, 0.0).astype(BF16)


def prepare(same, other, shard):
    places = same.shape[2] + other.shape[2]
    return call(
        prepare_kernel, shaped((places, shard), BF16), [VMEM] * 2, VMEM, moved=2 * places * shard
    )(same, other)


def update_kernel(steps, *refs):
    pieces = refs[: len(steps)]
    sender_ref, table_ref, sums_ref, new_table_ref, new_sums_ref, answer_ref, grad = refs[len(steps) :]
    replicas, columns = len(steps), pieces[0].shape[0]
    for step, piece in zip(steps, pieces):
        start = lax.rem(lax.axis_index("rep") + replicas - step, replicas) * columns
        grad[pl.ds(pl.multiple_of(start, columns), columns), :] = piece[...].astype(F32)
    whole = grad[...]
    sums = sums_ref[...] + jnp.mean(whole * whole, axis=0, keepdims=True)
    new_sums_ref[...] = sums
    step = whole * (LEARN_RATE * lax.rsqrt(sums))
    new_table = table_ref[...] - step.T
    new_table_ref[...] = new_table
    answer = product(sender_ref[...], new_table.astype(BF16)).astype(BF16)
    chips, cores, capacity = answer_ref.shape[:3]
    answer = answer.reshape(cores, chips, capacity, LANES)
    for core in range(cores):
        answer_ref[:, lax.rem(lax.axis_index("core") + core, cores)] = answer[core]


def update(steps, pieces, sender, table_rows, row_accumulators, cores, capacity):
    places, shard = sender.shape

    def kernel(*refs):
        update_kernel(steps, *refs)

    new_table, sums, answer = call(
        kernel,
        [
            pltpu.VMEM((shard, LANES), F32),
            pltpu.VMEM((1, shard), F32),
            shaped((places // (cores * capacity), cores, capacity, LANES), BF16),
        ],
        [VMEM] * (len(pieces) + 3),
        [VMEM] * 3,
        scratch=[pltpu.VMEM((LANES, shard), F32)],
        flops=2 * shard * places * LANES,
        moved=2 * places * (shard + LANES),
    )(*pieces, sender, table_rows, row_accumulators.reshape(1, shard))
    return new_table, sums.reshape(shard), answer


def unpack_kernel(places_ref, returned_ref, out_ref):
    matrix = places_ref[lax.axis_index("rep")]
    cores = returned_ref.shape[1]
    half = matrix.shape[1] // cores
    fresh = None
    for core in range(cores):
        rows = returned_ref[:, lax.rem(lax.axis_index("core") + core, cores)].reshape(half, LANES)
        added = product(matrix[:, core * half : (core + 1) * half], rows)
        fresh = added if fresh is None else fresh + added
    out_ref[...] = fresh.astype(BF16)


def unpack(matrices, returned):
    _, quarter, places = matrices.shape
    return call(
        unpack_kernel,
        shaped((quarter, LANES), BF16),
        [VMEM] * 2,
        VMEM,
        flops=2 * quarter * places * LANES,
        moved=2 * places * (quarter + LANES),
    )(matrices, returned)


def send(piece, step, replicas):
    return lax.ppermute(piece, "rep", [(i, (i + step) % replicas) for i in range(replicas)])


def send_order(replicas):
    return sorted(range(1, replicas), key=lambda step: -min(step, replicas - step))


def on_device(adjacency, grad_out, row_owner, table_slot, table_rows, row_accumulators):
    chips, cores = lax.axis_size("chip"), lax.axis_size("core")
    peers = chips * cores
    replicas = lax.axis_size("rep")
    rows = adjacency.shape[0]
    width = grad_out.shape[2]
    shard = table_rows.shape[0]
    quarter = rows // replicas
    capacity = max(2, 2 * quarter // peers)
    order = send_order(replicas)
    me = lax.axis_index("rep")

    columns, owner, slot = split(grad_out[0], row_owner, table_slot, replicas)
    pieces = [columns[0]] + [send(columns[step], step, replicas) for step in order]
    tile, places, slots, weight, mine = plan(
        adjacency, owner, slot, replicas, peers, cores, capacity
    )
    message = propagate(pieces, tile, places, slots, cores, capacity)

    landed = lax.all_to_all(message, "chip", split_axis=0, concat_axis=0, tiled=True)
    across = lax.ppermute(landed[:, 1:], "core", [(0, 1), (1, 0)])
    sums, same = accumulate(landed, weight, mine, shard)
    piece, other = accumulate(across, weight, mine, shard, before=sums)
    pieces = [piece] + [send(piece, step, replicas) for step in order]
    sender = prepare(same, other, shard)
    new_table, new_accumulators, answer = update(
        [0, *order], pieces, sender, table_rows, row_accumulators, cores, capacity
    )

    returned = lax.all_to_all(
        answer.reshape(peers, capacity, width),
        ("chip", "core"), split_axis=0, concat_axis=0, tiled=True,
    )
    fresh = unpack(places, returned.reshape(chips, cores, capacity, width))
    pieces = [send(fresh, step, replicas) for step in order]
    fresh_rows = jnp.zeros((rows, width), BF16)
    for step, piece in zip([0, *order], [fresh, *pieces]):
        source = lax.rem(me + replicas - step, replicas) * quarter
        fresh_rows = lax.dynamic_update_slice(fresh_rows, piece, (source, 0))
    return (new_table, new_accumulators, fresh_rows)


def solution(mesh):
    dom, replicas = mesh.devices.shape
    chips = Mesh(mesh.devices.reshape(dom // CORES, CORES, replicas), ("chip", "core", "rep"))
    split_rows = ("chip", "core")
    return jax.shard_map(
        on_device,
        mesh=chips,
        in_specs=(
            P(split_rows, None),
            P("rep", split_rows, None),
            P(split_rows, None),
            P(split_rows),
            P(split_rows, None),
            P(split_rows),
        ),
        out_specs=(P(split_rows, None), P(split_rows), P(split_rows, None)),
        check_vma=False,
    )
```

```python
import jax
import jax.numpy as jnp
from jax import lax
from jax.experimental import pallas as pl
from jax.experimental.pallas import tpu as pltpu
from jax.sharding import Mesh
from jax.sharding import PartitionSpec as P

LAYERS = 3
LEARN_RATE = 0.5
LANES = 128
SUBLANES = 8
PACKED = 16
CHUNKS = 4
CORES = 2
RADIX_BITS = 4
MEBI = 1024 * 1024

VMEM = pl.BlockSpec(memory_space=pltpu.VMEM)
HBM = pl.BlockSpec(memory_space=pltpu.HBM)
BF16 = jnp.bfloat16
F32 = jnp.float32


def ids(shape, axis):
    return lax.broadcasted_iota(jnp.int32, shape, axis)


def product(left, right):
    return jnp.dot(left, right, preferred_element_type=F32)


def shaped(shape, dtype):
    return jax.ShapeDtypeStruct(shape, dtype)


def call(kernel, out_shape, in_specs, out_specs, scratch=(), mebi=16, flops=0, moved=0):
    return pl.pallas_call(
        kernel,
        out_shape=out_shape,
        in_specs=in_specs,
        out_specs=out_specs,
        scratch_shapes=list(scratch),
        compiler_params=pltpu.CompilerParams(vmem_limit_bytes=mebi * MEBI),
        cost_estimate=pl.CostEstimate(flops=flops, bytes_accessed=moved, transcendentals=0),
    )


def split_kernel(grad_hbm, owner_hbm, slot_hbm, *refs):
    *pieces, owner, slot, grad, turned, arrived, lists_arrived = refs
    lists = [
        pltpu.make_async_copy(owner_hbm, owner, lists_arrived.at[0]),
        pltpu.make_async_copy(slot_hbm, slot, lists_arrived.at[1]),
    ]
    chunks = arrived.shape[0]
    depth = grad.shape[0] // chunks
    copies = []
    for chunk in range(chunks):
        part = pl.ds(chunk * depth, depth)
        copies.append(
            pltpu.make_async_copy(grad_hbm.at[part], grad.at[part], arrived.at[chunk])
        )
        copies[-1].start()
    for copy in lists:
        copy.start()
    for chunk in range(chunks):
        copies[chunk].wait()
        part = slice(chunk * depth, (chunk + 1) * depth)
        turned[:, part] = grad[part, :].T
    replicas, columns = len(pieces), pieces[0].shape[0]
    for step, piece in enumerate(pieces):
        start = lax.rem(lax.axis_index("rep") + step, replicas) * columns
        piece[...] = turned[pl.ds(pl.multiple_of(start, columns), columns), :]
    for copy in lists:
        copy.wait()


def split(grad, row_owner, table_slot, replicas):
    rows, width = grad.shape
    held = [grad, row_owner.reshape(1, rows), table_slot.reshape(1, rows)]
    *pieces, owner, slot = call(
        split_kernel,
        [shaped((width // replicas, rows), BF16)] * replicas
        + [pltpu.VMEM((1, rows), jnp.int32)] * 2,
        [HBM] * 3,
        [VMEM] * (replicas + 2),
        scratch=[
            pltpu.VMEM((rows, width), BF16),
            pltpu.VMEM((width, rows), BF16),
            pltpu.SemaphoreType.DMA((CHUNKS,)),
            pltpu.SemaphoreType.DMA((2,)),
        ],
    )(*[pltpu.with_memory_space_constraint(array, pltpu.HBM) for array in held])
    return pieces, owner, slot


def plan_kernel(
    capacity, cores, tile_hbm, owner_ref, slot_ref, tile_ref, places_ref, slots_ref, weight_ref, mine_ref, arrived
):
    tile_copy = pltpu.make_async_copy(tile_hbm, tile_ref, arrived)
    tile_copy.start()
    quarters, quarter, places = places_ref.shape
    peers = places // capacity
    square = (quarter, quarter)
    upper = jnp.where(ids(square, 0) <= ids(square, 1), 1.0, 0.0).astype(BF16)
    index = ids((LANES, quarter), 0)
    lane = ids(mine_ref.shape, 0)
    lists = None
    for number in range(quarters):
        lanes = slice(number * quarter, (number + 1) * quarter)
        named, slot = owner_ref[:, lanes], slot_ref[:, lanes]
        other = lax.rem(named + lax.axis_index("core"), cores)
        owner = other * (peers // cores) + lax.div(named, cores)
        hot = ids((peers, quarter), 0) == owner
        owner_hot = jnp.where(hot, 1.0, 0.0).astype(BF16)
        running = product(owner_hot, upper)
        rank = jnp.sum(jnp.where(hot, running, 0.0), axis=0, keepdims=True).astype(jnp.int32) - 1
        place = (owner * capacity + rank).astype(F32)
        column = jnp.broadcast_to(place, (LANES, quarter)).T.astype(jnp.int32)
        for part in range(places // LANES):
            here = column == ids(column.shape, 1) + part * LANES
            places_ref[number, :, part * LANES : (part + 1) * LANES] = jnp.where(
                here, 1.0, 0.0
            ).astype(BF16)
        high, low = slot >> RADIX_BITS, slot & ((1 << RADIX_BITS) - 1)
        first = number * capacity + rank
        spread = jnp.where(
            index == first, high, jnp.where(index == first + quarters * capacity, low, 0)
        )
        added = lax.dot_general(
            owner_hot,
            spread.astype(F32).astype(BF16),
            (((1,), (1,)), ((), ())),
            preferred_element_type=F32,
        )
        lists = added if lists is None else lists + added
        shape = weight_ref.shape[1:]
        lane, turn = ids(shape, 0), lax.rem(ids(shape, 1), capacity)
        turn = turn + number * capacity
        units = jnp.where(lane == turn + quarters * capacity, 1.0, 0.0)
        weight_ref[number] = jnp.where(lane == turn, float(1 << RADIX_BITS), units).astype(BF16)
    slots_ref[...] = lists.astype(BF16)
    mine = ids(mine_ref.shape, 0) == ids(mine_ref.shape, 1) // capacity
    mine_ref[...] = jnp.where(mine, 1.0, 0.0)
    tile_copy.wait()


def plan(adjacency, owner, slot, quarters, peers, cores, capacity):
    rows = slot.shape[1]
    places = peers * capacity

    def kernel(*refs):
        plan_kernel(capacity, cores, *refs)

    return call(
        kernel,
        [
            pltpu.VMEM(adjacency.shape, BF16),
            shaped((quarters, rows // quarters, places), BF16),
            shaped((peers, LANES), BF16),
            shaped((quarters, LANES, places // cores), BF16),
            shaped((peers // cores, places // cores), F32),
        ],
        [HBM, VMEM, VMEM],
        [VMEM] * 5,
        scratch=[pltpu.SemaphoreType.DMA],
    )(pltpu.with_memory_space_constraint(adjacency, pltpu.HBM), owner, slot)


def propagate_kernel(*refs):
    *pieces, tile_ref, places_ref, slots_ref, out_ref = refs
    total = pieces[0][...].astype(F32)
    for piece in pieces[1:]:
        total = total + piece[...].astype(F32)
    state = total.astype(BF16)
    columns = state.shape[0]
    quarters, quarter, _ = places_ref.shape
    for _ in range(LAYERS):
        full = jnp.concatenate([state] * (LANES // columns), axis=0)
        state = product(full, tile_ref[...])[:columns].astype(BF16)
        total = total + state.astype(F32)
    term = (total / F32(LAYERS + 1)).astype(BF16)
    full = jnp.concatenate(
        [term[:, number * quarter : (number + 1) * quarter] for number in range(quarters)], axis=0
    )
    packed = jnp.concatenate(
        [
            product(full, places_ref[number])[number * columns : (number + 1) * columns].astype(BF16)
            for number in range(quarters)
        ],
        axis=0,
    )
    chips, cores, pairs = out_ref.shape[:3]
    packed = packed.T.reshape(cores, chips, pairs - 1, 2, LANES)
    lists = slots_ref[...]
    for core in range(cores):
        out_ref[:, core, : pairs - 1] = packed[core]
        own = lists[core * chips : (core + 1) * chips]
        out_ref[:, core, pairs - 1] = jnp.broadcast_to(own[:, None, :], (chips, 2, LANES))


def propagate(pieces, tile, places, slots, cores, capacity):
    chips = slots.shape[0] // cores
    rows = tile.shape[0]
    return call(
        propagate_kernel,
        shaped((chips, cores, capacity // 2 + 1, 2, LANES), BF16),
        [VMEM] * (len(pieces) + 3),
        VMEM,
        flops=2 * LAYERS * rows * rows * LANES,
        moved=2 * rows * rows,
    )(*pieces, tile, places, slots)


def accumulate_kernel(shard, message_ref, weight_ref, mine_ref, *refs):
    *before, piece_ref, rows_ref = refs
    quarters, _, places = weight_ref.shape
    message = message_ref.at[:, 0]
    pairs = message.shape[1]
    columns = LANES // quarters
    digits = message[:, pairs - 1, 0, :]
    data = message[:, : pairs - 1].reshape(places, LANES)
    block = ids((shard, LANES), 1) // columns
    index = ids((shard, places), 0).astype(jnp.int16)
    slots = []
    for number in range(quarters):
        lists = product(digits, weight_ref[number])
        slots.append(jnp.sum(lists * mine_ref[...], axis=0, keepdims=True).astype(jnp.int32))
        rows_ref[number] = jnp.broadcast_to(slots[number], rows_ref.shape[1:])
    sums = None
    for number in range(quarters):
        wide = jnp.broadcast_to(slots[number], (PACKED, places)).astype(jnp.int16)
        hot = index == jnp.concatenate([wide] * (shard // PACKED), axis=0)
        receiver = jnp.where(hot, jnp.ones(hot.shape, BF16), jnp.zeros(hot.shape, BF16))
        added = product(receiver, data)
        sums = added if sums is None else jnp.where(block == number, added, sums)
    if before:
        piece = before[0][...] + sums
        turned = piece.T
        whole = turned[:columns]
        for number in range(1, quarters):
            whole = whole + turned[number * columns : (number + 1) * columns]
        piece_ref[...] = whole.astype(BF16)
    else:
        piece_ref[...] = sums


def accumulate(message, weight, mine, shard, before=None):
    quarters, _, places = weight.shape

    def kernel(*refs):
        accumulate_kernel(shard, *refs)

    piece = shaped((shard, LANES), F32)
    if before is not None:
        piece = shaped((LANES // quarters, shard), BF16)
    earlier = [] if before is None else [before]
    return call(
        kernel,
        [piece, shaped((quarters, SUBLANES, places), jnp.int32)],
        [VMEM] * (3 + len(earlier)),
        [VMEM] * 2,
        flops=2 * quarters * shard * places * LANES,
        moved=2 * places * (shard + LANES),
    )(message, weight, mine, *earlier)


def prepare_kernel(same_ref, other_ref, sender_ref):
    places, shard = sender_ref.shape
    me = lax.axis_index("rep")
    slot = jnp.concatenate([same_ref[me], other_ref[me]], axis=1).astype(F32)
    column = jnp.concatenate([slot] * (LANES // SUBLANES), axis=0).T.astype(jnp.int32)
    for part in range(shard // LANES):
        here = column == ids(column.shape, 1) + part * LANES
        sender_ref[:, part * LANES : (part + 1) * LANES] = jnp.where(here, 1.0, 0.0).astype(BF16)


def prepare(same, other, shard):
    places = same.shape[2] + other.shape[2]
    return call(
        prepare_kernel, shaped((places, shard), BF16), [VMEM] * 2, VMEM, moved=2 * places * shard
    )(same, other)


def update_kernel(steps, *refs):
    pieces = refs[: len(steps)]
    sender_ref, table_ref, sums_ref, new_table_ref, new_sums_ref, answer_ref, grad = refs[len(steps) :]
    replicas, columns = len(steps), pieces[0].shape[0]
    for step, piece in zip(steps, pieces):
        start = lax.rem(lax.axis_index("rep") + replicas - step, replicas) * columns
        grad[pl.ds(pl.multiple_of(start, columns), columns), :] = piece[...].astype(F32)
    whole = grad[...]
    sums = sums_ref[...] + jnp.mean(whole * whole, axis=0, keepdims=True)
    new_sums_ref[...] = sums
    step = whole * (LEARN_RATE * lax.rsqrt(sums))
    new_table = table_ref[...] - step.T
    new_table_ref[...] = new_table
    answer = product(sender_ref[...], new_table.astype(BF16)).astype(BF16)
    chips, cores, capacity = answer_ref.shape[:3]
    answer = answer.reshape(cores, chips, capacity, LANES)
    for core in range(cores):
        answer_ref[:, core] = answer[core]


def update(steps, pieces, sender, table_rows, row_accumulators, cores, capacity):
    places, shard = sender.shape

    def kernel(*refs):
        update_kernel(steps, *refs)

    new_table, sums, answer = call(
        kernel,
        [
            pltpu.VMEM((shard, LANES), F32),
            pltpu.VMEM((1, shard), F32),
            shaped((places // (cores * capacity), cores, capacity, LANES), BF16),
        ],
        [VMEM] * (len(pieces) + 3),
        [VMEM] * 3,
        scratch=[pltpu.VMEM((LANES, shard), F32)],
        flops=2 * shard * places * LANES,
        moved=2 * places * (shard + LANES),
    )(*pieces, sender, table_rows, row_accumulators.reshape(1, shard))
    return new_table, sums.reshape(shard), answer


def unpack_kernel(core, places_ref, returned_ref, *refs):
    *before, out_ref = refs
    half = returned_ref.shape[0] * returned_ref.shape[2]
    matrix = places_ref[lax.axis_index("rep"), :, core * half : (core + 1) * half]
    fresh = product(matrix, returned_ref[:, 0].reshape(half, LANES))
    if before:
        fresh = before[0][...] + fresh
    out_ref[...] = fresh.astype(out_ref.dtype)


def unpack(matrices, returned, core, before=None):
    _, quarter, places = matrices.shape

    def kernel(*refs):
        unpack_kernel(core, *refs)

    earlier = [] if before is None else [before]
    return call(
        kernel,
        shaped((quarter, LANES), F32 if before is None else BF16),
        [VMEM] * (2 + len(earlier)),
        VMEM,
        flops=quarter * places * LANES,
        moved=2 * places * (quarter + LANES),
    )(matrices, returned, *earlier)


def exchange(blocks):
    landed = lax.all_to_all(blocks, "chip", split_axis=0, concat_axis=0, tiled=True)
    return landed, lax.ppermute(landed[:, 1:], "core", [(0, 1), (1, 0)])


def send(piece, step, replicas):
    return lax.ppermute(piece, "rep", [(i, (i + step) % replicas) for i in range(replicas)])


def send_order(replicas):
    return sorted(range(1, replicas), key=lambda step: -min(step, replicas - step))


def on_device(adjacency, grad_out, row_owner, table_slot, table_rows, row_accumulators):
    chips, cores = lax.axis_size("chip"), lax.axis_size("core")
    peers = chips * cores
    replicas = lax.axis_size("rep")
    rows = adjacency.shape[0]
    width = grad_out.shape[2]
    shard = table_rows.shape[0]
    quarter = rows // replicas
    capacity = max(2, 2 * quarter // peers)
    order = send_order(replicas)
    me = lax.axis_index("rep")

    columns, owner, slot = split(grad_out[0], row_owner, table_slot, replicas)
    pieces = [columns[0]] + [send(columns[step], step, replicas) for step in order]
    tile, places, slots, weight, mine = plan(
        adjacency, owner, slot, replicas, peers, cores, capacity
    )
    message = propagate(pieces, tile, places, slots, cores, capacity)

    landed, across = exchange(message)
    sums, same = accumulate(landed, weight, mine, shard)
    piece, other = accumulate(across, weight, mine, shard, before=sums)
    pieces = [piece] + [send(piece, step, replicas) for step in order]
    sender = prepare(same, other, shard)
    new_table, new_accumulators, answer = update(
        [0, *order], pieces, sender, table_rows, row_accumulators, cores, capacity
    )

    landed, across = exchange(answer)
    fresh = unpack(places, landed, 0)
    fresh = unpack(places, across, 1, before=fresh)
    pieces = [send(fresh, step, replicas) for step in order]
    fresh_rows = jnp.zeros((rows, width), BF16)
    for step, piece in zip([0, *order], [fresh, *pieces]):
        source = lax.rem(me + replicas - step, replicas) * quarter
        fresh_rows = lax.dynamic_update_slice(fresh_rows, piece, (source, 0))
    return (new_table, new_accumulators, fresh_rows)


def solution(mesh):
    dom, replicas = mesh.devices.shape
    chips = Mesh(mesh.devices.reshape(dom // CORES, CORES, replicas), ("chip", "core", "rep"))
    split_rows = ("chip", "core")
    return jax.shard_map(
        on_device,
        mesh=chips,
        in_specs=(
            P(split_rows, None),
            P("rep", split_rows, None),
            P(split_rows, None),
            P(split_rows),
            P(split_rows, None),
            P(split_rows),
        ),
        out_specs=(P(split_rows, None), P(split_rows), P(split_rows, None)),
        check_vma=False,
    )
```
